32 devices in a mesh: dp: 4 (over z), fsdp: 8 (over y, x, core).
Axes of the slice: x: 2, y: 2, z: 4, core: 2. Of those that a mesh axis runs over, the one named last changes fastest.
Arguments:
- tokens: bfloat16 [64, 512, 768], P('dp', 'fsdp'), may hold values from -6 to 6
- cotangent: bfloat16 [64, 512, 768], P('dp', 'fsdp'), may hold values from -6 to 6
- key_mask: int32 [64, 512], P('dp', 'fsdp'), may hold values from 0 to 1, as said below
- seq_lengths: int32 [64], P(('dp', 'fsdp')), may hold values from 257 to 512, as said below
- block_pattern: int32 [12], replicated, may hold values from 0 to 1, as said below
- deal_order: int32 [4, 16], P('dp'), may hold values from 0 to 15, each once within a row
- qkv_weight: bfloat16 [768, 2304], P(('dp', 'fsdp')), may hold values from -0.21875 to 0.21875
- out_weight: bfloat16 [768, 768], P(('dp', 'fsdp')), may hold values from -2.5 to 2.5
- up_weight: bfloat16 [768, 3072], P(('dp', 'fsdp')), may hold values from -0.21875 to 0.21875
- down_weight: bfloat16 [3072, 768], P(('dp', 'fsdp')), may hold values from -0.109375 to 0.109375
- query_bias: bfloat16 [768], P(('dp', 'fsdp')), may hold values from -3 to 3
- value_bias: bfloat16 [768], P(('dp', 'fsdp')), may hold values from -0.29882812 to 0.29882812
- out_bias: bfloat16 [768], P(('dp', 'fsdp')), may hold values from -2 to 2
- up_bias: bfloat16 [3072], P(('dp', 'fsdp')), may hold values from -2 to 2
- down_bias: bfloat16 [768], P(('dp', 'fsdp')), may hold values from -2 to 2
- attn_gain: bfloat16 [768], P(('dp', 'fsdp')), may hold values from 0.5 to 1.5
- attn_shift: bfloat16 [768], P(('dp', 'fsdp')), may hold values from -1.1953125 to 1.1953125
- ffn_gain: bfloat16 [768], P(('dp', 'fsdp')), may hold values from 0.5 to 1.5
- ffn_shift: bfloat16 [768], P(('dp', 'fsdp')), may hold values from -1.1953125 to 1.1953125
Outputs:
- output: bfloat16 [64, 512, 768], P('dp', 'fsdp')
- grad_tokens: bfloat16 [64, 512, 768], P('dp', 'fsdp')
- grad_qkv_weight: float32 [768, 2304], P(('dp', 'fsdp'))
- grad_out_weight: float32 [768, 768], P(('dp', 'fsdp'))
- grad_up_weight: float32 [768, 3072], P(('dp', 'fsdp'))
- grad_down_weight: float32 [3072, 768], P(('dp', 'fsdp'))
- grad_query_bias: float32 [768], P(('dp', 'fsdp'))
- grad_value_bias: float32 [768], P(('dp', 'fsdp'))
- grad_out_bias: float32 [768], P(('dp', 'fsdp'))
- grad_up_bias: float32 [3072], P(('dp', 'fsdp'))
- grad_down_bias: float32 [768], P(('dp', 'fsdp'))
- grad_attn_gain: float32 [768], P(('dp', 'fsdp'))
- grad_attn_shift: float32 [768], P(('dp', 'fsdp'))
- grad_ffn_gain: float32 [768], P(('dp', 'fsdp'))
- grad_ffn_shift: float32 [768], P(('dp', 'fsdp'))
The draws below stay inside these ranges and needn't reach their ends.
Inputs may be any that keep to these rules, and one draw needn't show every extreme that they name: `key_mask`: positions 0 and 256 of every sequence are 1. `seq_lengths`: entry d * 2 + m is the length of the sequence dealt to micro-batch m of the device with index d over dp+fsdp. In each aligned block of 16 entries one is 512. `block_pattern`: both values occur. `deal_order`: each row holds each number once.
All inputs are finite; a program needn't handle non-finite values.
Results may differ from the reference program's by a relative error of at most 0.015.
Values may be sent and summed in bfloat16 or wider, within the bound.
No kernel may reach another device: no remote copies, remote signals or barrier semaphores. Data moves between devices by JAX's collectives and lax.ppermute only.
A program may use at most 192 MiB of HBM per device.

```python
import jax
import jax.numpy as jnp
from jax import lax

D = 768
H = 12
HD = 64
FF = 3072
SEQ = 512
MB = 2
GROUP_SEQS = 16
SEQS = 64
N_DP = 4
N_FSDP = 8


def draw_key_mask(key, part):
    key = jax.random.fold_in(key, 11)
    drawn_marks = (jax.random.randint(key, (SEQS, SEQ), 0, 8) != 0).astype(jnp.int32)
    columns = jnp.arange(SEQ, dtype=jnp.int32)[None, :]
    forced = (columns == 0) | (columns == SEQ // 2)
    return jnp.where(forced, 1, drawn_marks).astype(jnp.int32)


def draw_seq_lengths(key, part):
    key = jax.random.fold_in(key, 23)
    length_key, pick_key = jax.random.split(key)
    drawn = jax.random.randint(length_key, (N_DP, GROUP_SEQS), SEQ // 2 + 1, SEQ + 1)
    full_slot = jax.random.randint(pick_key, (N_DP, 1), 0, GROUP_SEQS)
    slots = jnp.arange(GROUP_SEQS, dtype=jnp.int32)[None, :]
    drawn = jnp.where(slots == full_slot, SEQ, drawn)
    groups = jnp.arange(N_DP, dtype=jnp.int32)[:, None]
    least_slot = (full_slot + 1) % GROUP_SEQS
    drawn = jnp.where((groups == 0) & (slots == least_slot), SEQ // 2 + 1, drawn)
    return drawn.reshape(SEQS).astype(jnp.int32)


def draw_block_pattern(key, part):
    key = jax.random.fold_in(key, 37)
    bit_key, order_key = jax.random.split(key)
    bits = jax.random.randint(bit_key, (H,), 0, 2)
    order = jax.random.permutation(order_key, H)
    heads = jnp.arange(H, dtype=jnp.int32)
    bits = jnp.where(heads == order[0], 0, bits)
    bits = jnp.where(heads == order[1], 1, bits)
    return bits.astype(jnp.int32)


def block_levels(stream_key, dims, shards, smallest, top_value):
    def one(axis_at, shards_of):
        steps = jax.random.uniform(jax.random.fold_in(jax.random.fold_in(stream_key, 6), axis_at), (shards_of,), jnp.float32, smallest / len(shards), top_value / len(shards))
        return jnp.repeat(jnp.exp(steps), dims[axis_at] // shards_of).reshape((-1,) + (1,) * (len(dims) - axis_at - 1))

    gain = one(*shards[0])
    for cut in shards[1:]:
        gain = gain * one(*cut)
    return gain


def normal_values(key, extent, width, limit, cuts=(), held_as=jnp.bfloat16):
    values = width * jax.random.normal(key, extent, jnp.float32)
    if cuts:
        values = values * block_levels(key, extent, cuts, -0.22, 0.18)
    return jnp.clip(values, -limit, limit).astype(held_as)


def setup_inputs(seed: int = 0) -> dict:
    key_of = jax.random.split(jax.random.key(seed), 20)
    return {
        "tokens": normal_values(key_of[0], (SEQS, SEQ, D), 1.0, 6.0, ((0, 4), (1, 8))),
        "cotangent": normal_values(key_of[1], (SEQS, SEQ, D), 1.0, 6.0, ((0, 4), (1, 8))),
        "key_mask": draw_key_mask(jax.random.fold_in(key_of[19], 71), 0),
        "seq_lengths": draw_seq_lengths(jax.random.fold_in(key_of[19], 71), 0),
        "block_pattern": draw_block_pattern(jax.random.fold_in(key_of[19], 71), 0),
        "deal_order": jax.vmap(lambda own: jax.random.permutation(own, GROUP_SEQS))(jax.random.split(key_of[5], N_DP)).reshape((N_DP, GROUP_SEQS)).astype(jnp.int32),
        "qkv_weight": normal_values(key_of[6], (D, 3 * D), D ** -0.5, 0.21875, ((0, 32),)),
        "out_weight": normal_values(key_of[7], (D, D), (D // 128) ** -0.5, 2.5, ((0, 32),)),
        "up_weight": normal_values(key_of[8], (D, FF), D ** -0.5, 0.21875, ((0, 32),)),
        "down_weight": normal_values(key_of[9], (FF, D), FF ** -0.5, 0.109375, ((0, 32),)),
        "query_bias": normal_values(key_of[10], (D,), 0.5, 3.0, ((0, 32),)),
        "value_bias": normal_values(key_of[11], (D,), 0.05, 0.29882812, ((0, 32),)),
        "out_bias": normal_values(key_of[12], (D,), 0.3, 2.0, ((0, 32),)),
        "up_bias": normal_values(key_of[13], (FF,), 0.3, 2.0, ((0, 32),)),
        "down_bias": normal_values(key_of[14], (D,), 0.3, 2.0, ((0, 32),)),
        "attn_gain": jnp.clip(1.0 + 0.1 * jax.random.normal(key_of[15], (D,), jnp.float32), 0.5, 1.5).astype(jnp.bfloat16),
        "attn_shift": normal_values(key_of[16], (D,), 0.2, 1.1953125, ((0, 32),)),
        "ffn_gain": jnp.clip(1.0 + 0.1 * jax.random.normal(key_of[17], (D,), jnp.float32), 0.5, 1.5).astype(jnp.bfloat16),
        "ffn_shift": normal_values(key_of[18], (D,), 0.2, 1.1953125, ((0, 32),)),
    }


PRECISE = lax.Precision.HIGHEST
EPSILON = 1e-12
NEGATIVE = -1e+30

@jax.custom_vjp
def low(v):
    return lax.optimization_barrier(v.astype(jnp.bfloat16)).astype(jnp.float32)

@jax.custom_vjp
def low_back(v):
    return v

def low_keep(v):
    return (low(v), None)

def low_pass(kept, grad):
    return (grad,)

def back_keep(v):
    return (v, None)

def back_low(kept, grad):
    return (low(grad),)
low.defvjp(low_keep, low_pass)
low_back.defvjp(back_keep, back_low)

def layer_norm(residual, scales, offset):
    centre = residual - lax.optimization_barrier(jnp.mean(residual, axis=-1, keepdims=True))
    spread = lax.optimization_barrier(jnp.mean(centre * centre, axis=-1, keepdims=True))
    return centre * lax.rsqrt(spread + EPSILON) * scales + offset

def sequence_forward(params, seq_rows, seq_marks, pattern):
    qkv_weight, out_weight, up_weight, down_weight, query_bias, value_bias, out_bias, up_bias, down_bias, attn_gain, attn_shift, ffn_gain, ffn_shift = params
    length_all = seq_rows.shape[0]
    half_len = length_all // 2
    model_width = out_weight.shape[0]
    bias_all = jnp.concatenate([query_bias, jnp.zeros_like(query_bias), value_bias])
    project = low(low_back(jnp.dot(seq_rows, qkv_weight, precision=PRECISE) + bias_all))
    queries = project[:, :model_width].reshape(2, half_len, H, HD)
    key_rows = project[:, model_width:2 * model_width].reshape(2, half_len, H, HD)
    values = project[:, 2 * model_width:].reshape(2, half_len, H, HD)
    swapped = block_flags(pattern)[None, None, :, None]
    keys_pair = jnp.where(swapped, key_rows[::-1], key_rows)
    values_pair = jnp.where(swapped, values[::-1], values)
    valid_blocks = seq_marks.reshape(2, half_len)
    valid_pair = jnp.where(block_flags(pattern)[None, :, None], valid_blocks[::-1][:, None, :], valid_blocks[:, None, :])
    scores = jnp.einsum('bqhd,bkhd->bhqk', queries, keys_pair, precision=PRECISE) * HD ** (-0.5)
    scores = low_back(scores)
    scores = jnp.where(valid_pair[:, :, None, :], scores, NEGATIVE)
    row_top = lax.optimization_barrier(jnp.max(scores, axis=-1, keepdims=True))
    exp_scores = jnp.exp(scores - row_top)
    attn_probs = low(exp_scores / lax.optimization_barrier(jnp.sum(exp_scores, axis=-1, keepdims=True)))
    mixed_heads = jnp.einsum('bhqk,bkhd->bqhd', attn_probs, values_pair, precision=PRECISE)
    mixed_heads = low(low_back(mixed_heads.reshape(length_all, model_width)))
    branch = low_back(jnp.dot(mixed_heads, out_weight, precision=PRECISE) + out_bias)
    hidden = layer_norm(seq_rows + branch, attn_gain, attn_shift)
    upward = low_back(jnp.dot(low(hidden), up_weight, precision=PRECISE) + up_bias)
    active = low(jax.nn.gelu(upward, approximate=False))
    ffn_branch = low_back(jnp.dot(active, down_weight, precision=PRECISE) + down_bias)
    return layer_norm(hidden + ffn_branch, ffn_gain, ffn_shift)

def block_flags(pattern):
    return pattern == 1

def group_forward(params, tokens_group, valid_group, pattern):

    def one_sequence(seq_rows, seq_marks):
        return sequence_forward(params, seq_rows, seq_marks, pattern)
    return jax.vmap(one_sequence)(tokens_group, valid_group)

def whole_forward(params, tokens_all, valid_all, pattern):
    count_all = tokens_all.shape[0]
    group_size = 4 if count_all % 4 == 0 else 1
    tokens_grouped = tokens_all.reshape(count_all // group_size, group_size, SEQ, D)
    valid_grouped = valid_all.reshape(count_all // group_size, group_size, SEQ)
    blockwise = jax.checkpoint(group_forward)

    def scan_step(scan_carry, pieces):
        return (scan_carry, blockwise(params, pieces[0], pieces[1], pattern))
    unused, outputs = lax.scan(scan_step, jnp.zeros((), jnp.float32), (tokens_grouped, valid_grouped))
    return outputs.reshape(count_all, SEQ, D)

def reference(tokens, cotangent, key_mask, seq_lengths, block_pattern, deal_order, qkv_weight, out_weight, up_weight, down_weight, query_bias, value_bias, out_bias, up_bias, down_bias, attn_gain, attn_shift, ffn_gain, ffn_shift):
    params = tuple((weight_item.astype(jnp.float32) for weight_item in (qkv_weight, out_weight, up_weight, down_weight, query_bias, value_bias, out_bias, up_bias, down_bias, attn_gain, attn_shift, ffn_gain, ffn_shift)))
    group_seqs = deal_order.shape[1]
    slot_ids = jnp.arange(group_seqs, dtype=jnp.int32)
    inverse = lax.optimization_barrier(jnp.sum(jnp.where(deal_order[:, :, None] == slot_ids[None, None, :], slot_ids[None, :, None], 0), axis=1)).astype(jnp.int32)
    groups = jnp.arange(N_DP, dtype=jnp.int32)[:, None]
    device = groups * N_FSDP + inverse % N_FSDP
    lengths_given = seq_lengths[(device * MB + inverse // N_FSDP).reshape(-1)]
    positions = jnp.arange(SEQ, dtype=jnp.int32)
    valid_all = (key_mask == 1) & (positions[None, :] < lengths_given[:, None])
    tokens_wide = tokens.astype(jnp.float32)

    def forward_all(params_in, tokens_in):
        return whole_forward(params_in, tokens_in, valid_all, block_pattern)
    outputs, backward = jax.vjp(forward_all, params, tokens_wide)
    grad_params, grad_input = backward(cotangent.astype(jnp.float32))
    return (outputs.astype(jnp.bfloat16), grad_input.astype(jnp.bfloat16), grad_params[0], grad_params[1], grad_params[2], grad_params[3], grad_params[4], grad_params[5], grad_params[6], grad_params[7], grad_params[8], grad_params[9], grad_params[10], grad_params[11], grad_params[12])
```

```python
import functools

import jax
import jax.numpy as jnp
from jax import lax
from jax.experimental import pallas as pl
from jax.experimental.pallas import tpu as pltpu
from jax.sharding import PartitionSpec as P

H = 12
HD = 64
EPSILON = 1e-12
NEGATIVE = -1e30
BF = jnp.bfloat16
F32 = jnp.float32
VMEM_LIMIT = 56 * 1024 * 1024
BOTH = ("dp", "fsdp")


def dot(a, b):
    return jnp.dot(a, b, preferred_element_type=F32)


def dot_nt(a, b):
    return lax.dot_general(a, b, (((1,), (1,)), ((), ())), preferred_element_type=F32)


def dot_tn(a, b):
    return lax.dot_general(a, b, (((0,), (0,)), ((), ())), preferred_element_type=F32)


def attention_fwd_kernel(heads, pattern, q_ref, k_ref, v_ref, valid_ref, mixed_ref, probs_ref):
    first = pl.program_id(1) * heads
    half = q_ref.shape[1] // 2
    for h in range(heads):
        pat = pattern[first + h]
        cols = slice(h * HD, (h + 1) * HD)
        for b in range(2):
            met = jnp.where(pat == 1, 1 - b, b)
            off = pl.multiple_of(met * half, half)
            q = q_ref[0, b * half : (b + 1) * half, cols] * jnp.asarray(HD ** (-0.5), BF)
            k = k_ref[0, pl.ds(off, half), cols]
            v = v_ref[0, pl.ds(off, half), cols]
            ok = valid_ref[0, met]
            scores = jnp.where(ok > 0.0, dot_nt(q, k), NEGATIVE)
            top = jnp.max(scores, axis=-1, keepdims=True)
            e = jnp.exp(scores - top)
            p = (e / jnp.sum(e, axis=-1, keepdims=True)).astype(BF)
            probs_ref[0, h, b] = p
            mixed_ref[0, b * half : (b + 1) * half, cols] = dot(p, v).astype(BF)


def attention_fwd(project, valid, pattern, heads=4):
    n, length, width3 = project.shape
    width = width3 // 3
    half = length // 2
    steps = H // heads
    wide = heads * HD

    def part(which):
        return pl.BlockSpec((1, length, wide), lambda s, g, pat: (s, 0, which * steps + g))

    return pl.pallas_call(
        functools.partial(attention_fwd_kernel, heads),
        grid_spec=pltpu.PrefetchScalarGridSpec(
            num_scalar_prefetch=1,
            grid=(n, steps),
            in_specs=[part(0), part(1), part(2), pl.BlockSpec((1, 2, 1, half), lambda s, g, pat: (s, 0, 0, 0))],
            out_specs=[
                pl.BlockSpec((1, length, wide), lambda s, g, pat: (s, 0, g)),
                pl.BlockSpec((1, heads, 2, half, half), lambda s, g, pat: (s, g, 0, 0, 0)),
            ],
        ),
        out_shape=[
            jax.ShapeDtypeStruct((n, length, width), BF),
            jax.ShapeDtypeStruct((n, H, 2, half, half), BF),
        ],
        compiler_params=pltpu.CompilerParams(vmem_limit_bytes=VMEM_LIMIT),
        cost_estimate=pl.CostEstimate(
            flops=4 * n * H * 2 * half * half * HD * 4, bytes_accessed=12_000_000, transcendentals=n * H * 2 * half * half
        ),
        name="attention_fwd",
    )(pattern, project, project, project, valid)


def attention_bwd_kernel(heads, pattern, q_ref, k_ref, v_ref, probs_ref, g_ref, dq_ref, dk_ref, dv_ref):
    first = pl.program_id(1) * heads
    half = q_ref.shape[1] // 2
    scale = HD ** (-0.5)
    for h in range(heads):
        pat = pattern[first + h]
        cols = slice(h * HD, (h + 1) * HD)
        for b in range(2):
            met = jnp.where(pat == 1, 1 - b, b)
            off = pl.multiple_of(met * half, half)
            rows = slice(b * half, (b + 1) * half)
            q = q_ref[0, rows, cols]
            g = g_ref[0, rows, cols]
            k = k_ref[0, pl.ds(off, half), cols]
            v = v_ref[0, pl.ds(off, half), cols]
            p = probs_ref[0, h, b]
            wide = p.astype(F32)
            gp = dot_nt(g, v)
            inner = jnp.sum(wide * gp, axis=-1, keepdims=True)
            gs = (wide * (gp - inner)).astype(BF)
            dq_ref[0, rows, cols] = (dot(gs, k) * scale).astype(BF)
            dk_ref[0, pl.ds(off, half), cols] = (dot_tn(gs, q) * scale).astype(BF)
            dv_ref[0, pl.ds(off, half), cols] = dot_tn(p, g).astype(BF)


def attention_bwd(project, probs, grad_mixed, pattern, heads=4):
    n, length, width3 = project.shape
    width = width3 // 3
    half = length // 2
    steps = H // heads
    wide = heads * HD

    def part(which):
        return pl.BlockSpec((1, length, wide), lambda s, g, pat: (s, 0, which * steps + g))

    out = pl.BlockSpec((1, length, wide), lambda s, g, pat: (s, 0, g))
    return pl.pallas_call(
        functools.partial(attention_bwd_kernel, heads),
        grid_spec=pltpu.PrefetchScalarGridSpec(
            num_scalar_prefetch=1,
            grid=(n, steps),
            in_specs=[
                part(0),
                part(1),
                part(2),
                pl.BlockSpec((1, heads, 2, half, half), lambda s, g, pat: (s, g, 0, 0, 0)),
                out,
            ],
            out_specs=[out, out, out],
        ),
        out_shape=[jax.ShapeDtypeStruct((n, length, width), BF)] * 3,
        compiler_params=pltpu.CompilerParams(vmem_limit_bytes=VMEM_LIMIT),
        cost_estimate=pl.CostEstimate(
            flops=8 * n * H * 2 * half * half * HD * 4, bytes_accessed=16_000_000, transcendentals=0
        ),
        name="attention_bwd",
    )(pattern, project, project, project, probs, grad_mixed)


def ffn_up_kernel(chunk, h_ref, w_ref, b_ref, act_ref, slope_ref):
    h = h_ref[...]
    for start in range(0, w_ref.shape[1], chunk):
        cols = slice(start, start + chunk)
        u = dot(h, w_ref[:, cols]) + b_ref[:, cols]
        phi = 0.5 + 0.5 * lax.erf(u * (2.0 ** -0.5))
        density = jnp.exp(-0.5 * u * u) * 0.3989422804014327
        act_ref[:, cols] = (u * phi).astype(BF)
        slope_ref[:, cols] = (phi + u * density).astype(BF)


def ffn_up(hidden_low, weight, bias, tile=256, chunk=512):
    rows, width = hidden_low.shape
    wide = weight.shape[1]
    out = pl.BlockSpec((tile, wide), lambda i: (i, 0))
    return pl.pallas_call(
        functools.partial(ffn_up_kernel, chunk),
        grid=(rows // tile,),
        in_specs=[
            pl.BlockSpec((tile, width), lambda i: (i, 0)),
            pl.BlockSpec((width, wide), lambda i: (0, 0)),
            pl.BlockSpec((1, wide), lambda i: (0, 0)),
        ],
        out_specs=[out, out],
        out_shape=[jax.ShapeDtypeStruct((rows, wide), BF)] * 2,
        compiler_params=pltpu.CompilerParams(vmem_limit_bytes=VMEM_LIMIT),
        cost_estimate=pl.CostEstimate(
            flops=2 * rows * width * wide + 40 * rows * wide, bytes_accessed=20_000_000, transcendentals=rows * wide
        ),
        name="ffn_up",
    )(hidden_low, weight, bias)


def plane_groups(size):
    return [list(range(c, size, 2)) for c in range(2)]


def core_swap(a):
    return lax.ppermute(a, "fsdp", [(i, i ^ 1) for i in range(lax.axis_size("fsdp"))])


def z_shift(a, k):
    n = lax.axis_size("dp")
    return lax.ppermute(a, "dp", [(i, (i + k) % n) for i in range(n)])


def z_gather(a):
    n = lax.axis_size("dp")
    me = lax.axis_index("dp")
    out = jnp.zeros((n, *a.shape), a.dtype)
    for k, part in enumerate([a] + [z_shift(a, k) for k in range(1, n)]):
        out = lax.dynamic_update_index_in_dim(out, part, lax.rem(me - k + n, n), 0)
    return out


def z_scatter(a):
    n = lax.axis_size("dp")
    me = lax.axis_index("dp")
    total = lax.dynamic_index_in_dim(a, me, 0, False).astype(F32)
    for k in range(1, n):
        total = total + z_shift(lax.dynamic_index_in_dim(a, lax.rem(me + k, n), 0, False), k).astype(F32)
    return total


def after(a, *earlier):
    return lax.optimization_barrier((a, *earlier))[0]


def plane_exchange(a):
    return lax.all_to_all(a, "fsdp", 0, 0, tiled=True, axis_index_groups=plane_groups(lax.axis_size("fsdp")))


def plane_gather(a):
    n = lax.axis_size("fsdp") // 2
    return plane_exchange(jnp.broadcast_to(a[None], (n, *a.shape)))


def core_order(core, own, other, axis):
    return jnp.where(core == 0, jnp.concatenate([own, other], axis), jnp.concatenate([other, own], axis))


def assemble(core, own, oth):
    own, oth = (jnp.transpose(a, (1, 0, 2, 3)).reshape(-1, a.shape[3]) for a in (own, oth))
    return core_order(core, own, oth, 1)


def half_of(a, which):
    wide = a.shape[1] // 2
    return lax.dynamic_slice_in_dim(a, which * wide, wide, 1)


class Gathered:
    def __init__(self, core, qkv, out, up, down, vectors):
        self.core = core
        self.rows = qkv.shape[0]
        self.widths = [w.shape[1] // 2 for w in (qkv, out, up)]
        self.size = vectors.shape[0]
        sides = jnp.stack(
            [
                jnp.concatenate([w[:, h * n : (h + 1) * n] for w, n in zip((qkv, out, up), self.widths)], 1)
                for h in range(2)
            ]
        )
        own = lax.dynamic_index_in_dim(sides, core, 0, False)
        chip = core_order(core, own, core_swap(lax.dynamic_index_in_dim(sides, 1 - core, 0, False)), 0)
        self.down = core_order(core, half_of(down, core), core_swap(half_of(down, 1 - core)), 0)
        vector_rows = jnp.zeros((8, self.widths[0]), BF).at[0, : self.size].set(vectors)
        self.first = jnp.concatenate([chip[:, : self.widths[0]], vector_rows], 0)
        self.second = chip[:, self.widths[0] :]

    def take_first(self, mine):
        other = core_swap(mine)
        rows = 2 * self.rows
        weight = assemble(self.core, mine[:, :, :rows], other[:, :, :rows])
        mine, other = (a[:, :, rows, : self.size] for a in (mine, other))
        every = jnp.where(self.core == 0, jnp.stack([mine, other], 2), jnp.stack([other, mine], 2))
        return weight, jnp.transpose(every, (1, 0, 2, 3)).reshape(-1, self.size)

    def take_second(self, mine):
        other = core_swap(mine)
        cut = self.widths[1]
        return (
            assemble(self.core, mine[..., :cut], other[..., :cut]),
            assemble(self.core, mine[..., cut:], other[..., cut:]),
        )

    def take_down(self, mine):
        mine = mine.reshape(-1, mine.shape[-1])
        return core_order(self.core, mine, core_swap(mine), 1)


def finish(core, total):
    rows = total.shape[0] // 2
    own = lax.dynamic_slice_in_dim(total, core * rows, rows, 0)
    other = core_swap(lax.dynamic_slice_in_dim(total, (1 - core) * rows, rows, 0))
    return core_order(core, own, other, 1)


def chip_parts(core, left, right):
    part = dot_tn(left, half_of(right, 1 - core)).astype(BF)

    def rest(left, right, sent):
        return (dot_tn(left, half_of(right, core)) + sent.astype(F32)).astype(BF)

    return part, rest


def summed(a):
    return jnp.sum(a.astype(F32), axis=0)


def by_plane(part):
    depth, plane = lax.axis_size("dp"), lax.axis_size("fsdp") // 2
    return jnp.transpose(part.reshape(depth, plane, -1, part.shape[1]), (1, 0, 2, 3))


def norm(residual):
    centre = residual - jnp.mean(residual, axis=-1, keepdims=True)
    scale = lax.rsqrt(jnp.mean(centre * centre, axis=-1, keepdims=True) + EPSILON)
    return centre * scale, scale


def norm_back(normed, scale, gained):
    inner = jnp.mean(gained * normed, axis=-1, keepdims=True)
    return scale * (gained - jnp.mean(gained, axis=-1, keepdims=True) - normed * inner)


def local(tokens, cotangent, key_mask, seq_lengths, block_pattern, deal_order, *shards):
    qkv_s, out_s, up_s, down_s = shards[:4]
    fsdp = lax.axis_size("fsdp")
    devices = fsdp * lax.axis_size("dp")
    me = lax.axis_index("fsdp")
    core = lax.rem(me, 2)
    count, piece, width = tokens.shape
    per = count // fsdp
    length = piece * fsdp
    fast = (2 * qkv_s.shape[0]) % 16 == 0

    def deal(a):
        return lax.all_to_all(a, "fsdp", split_axis=0, concat_axis=1, tiled=True)

    def give(a):
        return lax.all_to_all(a, "fsdp", split_axis=1, concat_axis=0, tiled=True)

    marks = key_mask.reshape(fsdp, per * piece)
    lengths = jnp.broadcast_to(seq_lengths[None], (fsdp, seq_lengths.shape[0]))
    notes = lax.all_to_all(jnp.concatenate([marks, lengths], 1), "fsdp", 0, 0, tiled=True)
    marks = notes[:, : per * piece].reshape(fsdp, per, piece).transpose(1, 0, 2).reshape(per, length)
    by_slot = notes[:, per * piece :].T.reshape(-1)
    own_ids = me * per + jnp.arange(per, dtype=jnp.int32)
    own_lengths = jnp.sum(jnp.where(deal_order[0][None, :] == own_ids[:, None], by_slot[None, :], 0), axis=1)
    positions = jnp.arange(length, dtype=jnp.int32)
    valid = ((marks == 1) & (positions[None, :] < own_lengths[:, None])).astype(F32)
    valid = valid.reshape(per, 2, 1, length // 2)

    vectors = jnp.concatenate(shards[4:])
    if fast:
        coming = Gathered(core, qkv_s, out_s, up_s, down_s, vectors)
        x3 = deal(tokens)
        first = z_gather(coming.first)
        second = z_gather(coming.second)
        first = plane_gather(after(first, x3))
        down = plane_gather(after(coming.down, first))
        down_w = coming.take_down(z_gather(down))
        second = plane_gather(after(second, down))
        g3 = deal(after(cotangent, second))
        qkv_w, every = coming.take_first(first)
        out_w, up_w = coming.take_second(second)
    else:
        x3 = deal(tokens)
        g3 = deal(cotangent)
        qkv_w, out_w, up_w, down_w, every = (
            lax.all_gather(w, BOTH, axis=0, tiled=True) for w in (qkv_s, out_s, up_s, down_s, vectors[None])
        )
    x = x3.reshape(per * length, width)
    sizes = [s.shape[0] for s in shards[4:]]
    starts = [sum(sizes[:i]) for i in range(len(sizes))]
    query_b, value_b, out_b, up_b, down_b, attn_gain, attn_shift, ffn_gain, ffn_shift = (
        every[:, a : a + n].astype(F32).reshape(1, -1) for a, n in zip(starts, sizes)
    )

    bias_all = jnp.concatenate([query_b, jnp.zeros_like(query_b), value_b], 1)
    project = (dot(x, qkv_w) + bias_all).astype(BF).reshape(per, length, 3 * width)
    mixed, probs = attention_fwd(project, valid, block_pattern)
    mixed = mixed.reshape(per * length, width)
    normed_one, scale_one = norm(x.astype(F32) + dot(mixed, out_w) + out_b)
    hidden = normed_one * attn_gain + attn_shift
    hidden_low = hidden.astype(BF)
    active, slope = ffn_up(hidden_low, up_w, up_b)
    normed_two, scale_two = norm(hidden + dot(active, down_w) + down_b)
    output = (normed_two * ffn_gain + ffn_shift).astype(BF).reshape(per, length, width)
    if fast:
        output = after(output, g3)
    output = give(output)

    g = g3.reshape(per * length, width).astype(F32)
    grad_ffn_gain = jnp.sum(g * normed_two, axis=0)
    grad_ffn_shift = jnp.sum(g, axis=0)
    grad_two = norm_back(normed_two, scale_two, g * ffn_gain)
    down_low = grad_two.astype(BF)
    grad_down_b = jnp.sum(down_low, axis=0, dtype=F32)

    if fast:
        part, rest = chip_parts(core, active, down_low)
        down_low = after(down_low, part)
        part = rest(active, down_low, core_swap(part))
        down_low = after(down_low, part)
        depth, plane = devices // fsdp, fsdp // 2
        down_part = z_scatter(part.reshape(depth, plane, -1, part.shape[1])).astype(BF)
    else:
        grad_down_w = dot_tn(active, down_low)
    up_low = (dot_nt(down_low, down_w) * slope.astype(F32)).astype(BF)
    grad_up_b = jnp.sum(up_low, axis=0, dtype=F32)
    if fast:
        part, rest = chip_parts(core, hidden_low, up_low)
        up_low = after(up_low, part)
        part = rest(hidden_low, up_low, core_swap(part))
        up_low = after(up_low, part)
        up_part = plane_exchange(after(by_plane(part), output))
        grad_up_w = finish(core, z_scatter(summed(up_part).astype(BF)))
    else:
        grad_up_w = dot_tn(hidden_low, up_low)
    grad_hidden = grad_two + dot_nt(up_low, up_w)
    grad_attn_gain = jnp.sum(grad_hidden * normed_one, axis=0)
    grad_attn_shift = jnp.sum(grad_hidden, axis=0)
    grad_one = norm_back(normed_one, scale_one, grad_hidden * attn_gain)
    out_low = grad_one.astype(BF)
    grad_out_b = jnp.sum(out_low, axis=0, dtype=F32)
    if fast:
        part, rest = chip_parts(core, mixed, out_low)
        out_low = after(out_low, part)
        part = rest(mixed, out_low, core_swap(part))
        out_low = after(out_low, part)
        out_part = plane_exchange(after(by_plane(part), up_part))
        grad_out_w = finish(core, z_scatter(summed(out_part).astype(BF)))
        down_part = plane_exchange(after(down_part, out_part))
        grad_down_w = finish(core, summed(down_part))
    else:
        grad_out_w = dot_tn(mixed, out_low)
    grad_mixed = dot_nt(out_low, out_w).astype(BF).reshape(per, length, width)
    grads = attention_bwd(project, probs, grad_mixed, block_pattern)
    grad_project = jnp.concatenate([d.reshape(per * length, width) for d in grads], 1)
    bias_sums = jnp.sum(grad_project, axis=0, dtype=F32)
    grad_vectors = (
        bias_sums[:width],
        bias_sums[2 * width :],
        grad_out_b,
        grad_up_b,
        grad_down_b,
        grad_attn_gain,
        grad_attn_shift,
        grad_ffn_gain,
        grad_ffn_shift,
    )
    laid = jnp.concatenate([v.reshape(devices, -1) for v in grad_vectors], 1)
    if fast:
        part, rest = chip_parts(core, x, grad_project)
        grad_project = after(grad_project, part)
        part = rest(x, grad_project, core_swap(part))
        grad_project = after(grad_project, part)
        laid = laid.reshape(depth * plane, 2, -1)
        sent = core_swap(lax.dynamic_index_in_dim(laid, 1 - core, 1, False).astype(BF))
        laid = lax.dynamic_index_in_dim(laid, core, 1, False) + sent.astype(F32)
        wide = part.shape[1]
        rows = jnp.zeros((depth * plane, 8, wide), BF).at[:, 0, : laid.shape[1]].set(laid.astype(BF))
        part = jnp.concatenate([part.reshape(depth * plane, -1, wide), rows], 1).reshape(-1, wide)
        qkv_part = plane_exchange(after(by_plane(part), down_part))
        total = z_scatter(summed(qkv_part).astype(BF))
        grad_qkv_w = finish(core, total[:-8])
        vector = total[-8, : laid.shape[1]]
    else:
        grad_qkv_w = dot_tn(x, grad_project)
        grad_qkv_w, grad_out_w, grad_up_w, grad_down_w, vector = (
            lax.psum_scatter(w.astype(BF), BOTH, scatter_dimension=0, tiled=True).astype(F32)
            for w in (grad_qkv_w, grad_out_w, grad_up_w, grad_down_w, laid)
        )
        vector = vector.reshape(-1)
    grad_tokens = (grad_one + dot_nt(grad_project, qkv_w)).astype(BF).reshape(per, length, width)
    if fast:
        grad_tokens = after(grad_tokens, qkv_part)
    grad_tokens = give(grad_tokens)
    vectors_out = [vector[a : a + n] for a, n in zip(starts, sizes)]
    return (output, grad_tokens, grad_qkv_w, grad_out_w, grad_up_w, grad_down_w, *vectors_out)


def solution(mesh):
    rows = P(BOTH, None)
    vec = P(BOTH)
    in_specs = (
        P("dp", "fsdp", None),
        P("dp", "fsdp", None),
        P("dp", "fsdp"),
        vec,
        P(),
        P("dp", None),
        *([rows] * 4),
        *([vec] * 9),
    )
    out_specs = (P("dp", "fsdp", None), P("dp", "fsdp", None), *([rows] * 4), *([vec] * 9))
    return jax.shard_map(local, mesh=mesh, in_specs=in_specs, out_specs=out_specs, check_vma=False)
```

```python
import functools

import jax
import jax.numpy as jnp
from jax import lax
from jax.experimental import pallas as pl
from jax.experimental.pallas import tpu as pltpu
from jax.sharding import PartitionSpec as P

H = 12
HD = 64
EPSILON = 1e-12
NEGATIVE = -1e30
BF = jnp.bfloat16
F32 = jnp.float32
VMEM_LIMIT = 56 * 1024 * 1024
BOTH = ("dp", "fsdp")
WEIGHT = 1


def dot(a, b):
    return jnp.dot(a, b, preferred_element_type=F32)


def dot_nt(a, b):
    return lax.dot_general(a, b, (((1,), (1,)), ((), ())), preferred_element_type=F32)


def dot_tn(a, b):
    return lax.dot_general(a, b, (((0,), (0,)), ((), ())), preferred_element_type=F32)


def whole(shape):
    return pl.BlockSpec(shape, lambda *_: (0,) * len(shape), pipeline_mode=pl.Buffered(1))


def params():
    return pltpu.CompilerParams(vmem_limit_bytes=VMEM_LIMIT)


def cost(flops, size, exps=0):
    return pl.CostEstimate(flops=int(flops * WEIGHT), bytes_accessed=int(size * WEIGHT), transcendentals=int(exps * WEIGHT))


class Pieces:
    def __init__(self, halves, spots, rows):
        self.halves, self.spots, self.rows = halves, spots, rows

    def arrays(self):
        return [a for half in self.halves for a in half]

    def specs(self):
        return [whole(a.shape) for a in self.arrays()]

    def put(self, place, refs, start, wide, out_ref):
        core, plane_at, depth_at, plane, depth = place
        each = len(refs) // 2
        for side, part in ((core, refs[:each]), (1 - core, refs[each:])):
            cols = pl.ds(pl.multiple_of(side * wide, 128), wide)
            for ref, spots in zip(part, self.spots):
                for i, (away, back) in enumerate(spots):
                    chip = lax.rem(depth_at + depth - back, depth) * plane + (plane_at ^ away)
                    rows = pl.ds(pl.multiple_of(chip * self.rows, 16), self.rows)
                    out_ref[rows, cols] = ref[i, :, start : start + wide]


def without(kernel, first, count):
    return lambda *refs: kernel(*refs[:first], *refs[first + count :])


def anywhere(arrays):
    return [pl.BlockSpec(memory_space=pl.ANY)] * len(arrays)


def tie(a, *earlier):
    return pl.pallas_call(
        lambda *refs: None,
        in_specs=anywhere((a, *earlier)),
        out_specs=pl.BlockSpec(memory_space=pl.ANY),
        out_shape=jax.ShapeDtypeStruct(a.shape, a.dtype),
        input_output_aliases={0: 0},
        compiler_params=params(),
        cost_estimate=cost(0, 0),
        name="tie",
    )(a, *earlier)


def place_of(place_ref, plane, depth):
    return place_ref[0], place_ref[1], place_ref[2], plane, depth


def load_weight(pieces, sizes, place_ref, refs, start, wide, out_ref):
    if pieces is None:
        out_ref[...] = refs[0][:, start : start + out_ref.shape[1]]
    else:
        pieces.put(place_of(place_ref, *sizes), refs, start, wide, out_ref)


def attention_kernel(pieces, sizes, n_pieces, place_ref, pattern, x_ref, b_ref, valid_ref, *refs):
    w_in, (project_ref, mixed_ref, probs_ref, w_ref) = refs[:n_pieces], refs[n_pieces:]
    width = x_ref.shape[2]
    half = x_ref.shape[1] // 2

    @pl.when(pl.program_id(0) == 0)
    def _():
        load_weight(pieces, sizes, place_ref, w_in, 0, 3 * width // 2, w_ref)

    x = x_ref[0]
    for part in range(3):
        cols = slice(part * width, (part + 1) * width)
        value = dot(x, w_ref[:, cols]) + b_ref[:, cols]
        project_ref[0, :, cols] = value.astype(BF)
    lanes = lax.broadcasted_iota(jnp.int32, (half, 2 * HD), 1) < HD

    def pair(i, carry):
        base = i * (2 * HD)
        for b in range(2):
            rows = pl.ds(b * half, half)
            q = project_ref[0, rows, pl.ds(pl.multiple_of(base, 128), 2 * HD)] * jnp.asarray(HD ** (-0.5), BF)
            outs = []
            for h in range(2):
                met = jnp.where(pattern[2 * i + h] == 1, 1 - b, b)
                off = pl.ds(pl.multiple_of(met * half, half), half)
                k = project_ref[0, off, pl.ds(pl.multiple_of(width + base, 128), 2 * HD)]
                v = project_ref[0, off, pl.ds(pl.multiple_of(2 * width + base, 128), 2 * HD)]
                own = jnp.where(lanes if h == 0 else jnp.logical_not(lanes), q, jnp.zeros_like(q))
                scores = jnp.where(valid_ref[0, met] > 0.0, dot_nt(own, k), NEGATIVE)
                e = jnp.exp(scores - jnp.max(scores, axis=-1, keepdims=True))
                p = (e * (1.0 / jnp.sum(e, axis=-1, keepdims=True))).astype(BF)
                probs_ref[0, 2 * i + h, b] = p
                outs.append(dot(p, v))
            mixed_ref[0, rows, pl.ds(pl.multiple_of(base, 128), 2 * HD)] = jnp.where(lanes, *outs).astype(BF)
        return carry

    lax.fori_loop(0, H // 2, pair, 0)


def qkv_attention(place, pattern, x3, bias, valid, pieces, sizes):
    n, length, width = x3.shape
    half = length // 2
    arrays = pieces.arrays() if isinstance(pieces, Pieces) else [pieces]
    specs = [whole(a.shape) for a in arrays]
    units = n * H * 2 * half * half
    return pl.pallas_call(
        functools.partial(
            attention_kernel, pieces if isinstance(pieces, Pieces) else None, sizes, len(arrays)
        ),
        grid_spec=pltpu.PrefetchScalarGridSpec(
            num_scalar_prefetch=2,
            grid=(n,),
            in_specs=[
                pl.BlockSpec((1, length, width), lambda s, *_: (s, 0, 0)),
                whole((1, 3 * width)),
                pl.BlockSpec((1, 2, 1, half), lambda s, *_: (s, 0, 0, 0)),
                *specs,
            ],
            out_specs=[
                pl.BlockSpec((1, length, 3 * width), lambda s, *_: (s, 0, 0)),
                pl.BlockSpec((1, length, width), lambda s, *_: (s, 0, 0)),
                pl.BlockSpec((1, H, 2, half, half), lambda s, *_: (s, 0, 0, 0, 0)),
                whole((width, 3 * width)),
            ],
        ),
        out_shape=[
            jax.ShapeDtypeStruct((n, length, 3 * width), BF),
            jax.ShapeDtypeStruct((n, length, width), BF),
            jax.ShapeDtypeStruct((n, H, 2, half, half), BF),
            jax.ShapeDtypeStruct((width, 3 * width), BF),
        ],
        compiler_params=params(),
        cost_estimate=cost(6 * n * length * width * width + 4 * units * HD * 4, 22e6, units),
        name="qkv_attention",
    )(place, pattern, x3, bias, valid, *arrays)


def norm(residual):
    centre = residual - jnp.mean(residual, axis=-1, keepdims=True)
    scale = lax.rsqrt(jnp.mean(centre * centre, axis=-1, keepdims=True) + EPSILON)
    return centre * scale, scale


def norm_back(normed, scale, gained):
    inner = jnp.mean(gained * normed, axis=-1, keepdims=True)
    return scale * (gained - jnp.mean(gained, axis=-1, keepdims=True) - normed * inner)


def up_kernel(chunk, mixed_ref, x_ref, vec_ref, up_b_ref, out_w_ref, *refs):
    up_w, (normed_ref, scale_ref, low_ref, act_ref, slope_ref) = refs[:-5], refs[-5:]
    width = x_ref.shape[1]
    normed, scale = norm(x_ref[...].astype(F32) + dot(mixed_ref[...], out_w_ref[...]) + vec_ref[0:1])
    normed_ref[...] = normed
    scale_ref[...] = scale
    low = (normed * vec_ref[1:2] + vec_ref[2:3]).astype(BF)
    low_ref[...] = low
    for j, up_w_ref in enumerate(up_w):
        for start in range(0, width, chunk):
            cols = slice(j * width + start, j * width + start + chunk)
            u = dot(low, up_w_ref[:, start : start + chunk]) + up_b_ref[:, cols]
            phi = 0.5 + 0.5 * lax.erf(u * (2.0 ** -0.5))
            density = jnp.exp(-0.5 * u * u) * 0.3989422804014327
            act_ref[:, cols] = (u * phi).astype(BF)
            slope_ref[:, cols] = (phi + u * density).astype(BF)


def rows_of(tile, width):
    return pl.BlockSpec((tile, width), lambda i, *_: (i, 0))


def out_up(mixed, x, vecs, up_b, out_w, up_w, tile=256, chunk=384):
    rows, width = x.shape
    wide = up_b.shape[1]
    return pl.pallas_call(
        functools.partial(up_kernel, chunk),
        grid=(rows // tile,),
        in_specs=[
            rows_of(tile, width),
            rows_of(tile, width),
            *[whole(a.shape) for a in (vecs, up_b, out_w, *up_w)],
        ],
        out_specs=[
            rows_of(tile, width),
            rows_of(tile, 1),
            rows_of(tile, width),
            rows_of(tile, wide),
            rows_of(tile, wide),
        ],
        out_shape=[
            jax.ShapeDtypeStruct((rows, width), F32),
            jax.ShapeDtypeStruct((rows, 1), F32),
            jax.ShapeDtypeStruct((rows, width), BF),
            jax.ShapeDtypeStruct((rows, wide), BF),
            jax.ShapeDtypeStruct((rows, wide), BF),
        ],
        compiler_params=params(),
        cost_estimate=cost(2 * rows * width * (width + wide), 38e6, rows * wide),
        name="out_up",
    )(mixed, x, vecs, up_b, out_w, *up_w)


def down_kernel(act_ref, slope_ref, normed_ref, g_ref, vec_ref, w_ref, *refs):
    out_ref, two_ref, down_low_ref, up_low_ref, sums_ref, up_sum_ref = refs
    width = g_ref.shape[1]

    @pl.when(pl.program_id(0) == 0)
    def _():
        sums_ref[...] = jnp.zeros_like(sums_ref)
        up_sum_ref[...] = jnp.zeros_like(up_sum_ref)

    hidden = normed_ref[...] * vec_ref[0:1] + vec_ref[1:2]
    normed, scale = norm(hidden + dot(act_ref[...], w_ref[...]) + vec_ref[2:3])
    out_ref[...] = (normed * vec_ref[3:4] + vec_ref[4:5]).astype(BF).reshape(out_ref.shape)
    g = g_ref[...].astype(F32)
    two = norm_back(normed, scale, g * vec_ref[3:4])
    two_ref[...] = two
    low = two.astype(BF)
    down_low_ref[...] = low
    sums_ref[0:1] += jnp.sum(g * normed, axis=0, keepdims=True)
    sums_ref[1:2] += jnp.sum(g, axis=0, keepdims=True)
    sums_ref[2:3] += jnp.sum(low.astype(F32), axis=0, keepdims=True)
    for start in range(0, w_ref.shape[0], width):
        cols = slice(start, start + width)
        up_low = (dot_nt(low, w_ref[cols, :]) * slope_ref[:, cols].astype(F32)).astype(BF)
        up_low_ref[:, cols] = up_low
        up_sum_ref[:, cols] += jnp.sum(up_low.astype(F32), axis=0, keepdims=True)


def given(tile, piece, length, width):
    return pl.BlockSpec(
        (tile // piece, 1, piece, width), lambda i, *_: (lax.rem(i, length // tile), i // (length // tile), 0, 0)
    )


def down_and_back(active, slope, normed, g, vecs, down_w, piece, length, tile=256):
    rows, width = g.shape
    wide = active.shape[1]
    return pl.pallas_call(
        down_kernel,
        grid=(rows // tile,),
        in_specs=[
            rows_of(tile, wide),
            rows_of(tile, wide),
            rows_of(tile, width),
            rows_of(tile, width),
            whole(vecs.shape),
            whole(down_w.shape),
        ],
        out_specs=[
            given(tile, piece, length, width),
            rows_of(tile, width),
            rows_of(tile, width),
            rows_of(tile, wide),
            whole((8, width)),
            whole((1, wide)),
        ],
        out_shape=[
            jax.ShapeDtypeStruct((length // piece, rows // length, piece, width), BF),
            jax.ShapeDtypeStruct((rows, width), F32),
            jax.ShapeDtypeStruct((rows, width), BF),
            jax.ShapeDtypeStruct((rows, wide), BF),
            jax.ShapeDtypeStruct((8, width), F32),
            jax.ShapeDtypeStruct((1, wide), F32),
        ],
        compiler_params=params(),
        cost_estimate=cost(4 * rows * width * wide, 38e6),
        name="down_and_back",
    )(active, slope, normed, g, vecs, down_w)


def up_back_kernel(up_low_ref, two_ref, normed_ref, scale_ref, gain_ref, out_w_ref, *refs):
    up_w, (one_ref, low_ref, mixed_ref, sums_ref) = refs[:-4], refs[-4:]
    width = two_ref.shape[1]

    @pl.when(pl.program_id(0) == 0)
    def _():
        sums_ref[...] = jnp.zeros_like(sums_ref)

    hidden = two_ref[...]
    for j, up_w_ref in enumerate(up_w):
        hidden = hidden + dot_nt(up_low_ref[:, j * width : (j + 1) * width], up_w_ref[...])
    normed = normed_ref[...]
    one = norm_back(normed, scale_ref[...], hidden * gain_ref[...])
    one_ref[...] = one
    low = one.astype(BF)
    low_ref[...] = low
    mixed_ref[...] = dot_nt(low, out_w_ref[...]).astype(BF)
    sums_ref[0:1] += jnp.sum(hidden * normed, axis=0, keepdims=True)
    sums_ref[1:2] += jnp.sum(hidden, axis=0, keepdims=True)
    sums_ref[2:3] += jnp.sum(low.astype(F32), axis=0, keepdims=True)


def up_back(up_low, two, normed, scale, gain, out_w, up_w, earlier, tile=256):
    rows, wide = up_low.shape
    width = two.shape[1]
    narrow = rows_of(tile, width)
    return pl.pallas_call(
        without(up_back_kernel, 6 + len(up_w), len(earlier)),
        grid=(rows // tile,),
        in_specs=[
            rows_of(tile, wide),
            narrow,
            narrow,
            rows_of(tile, 1),
            *[whole(a.shape) for a in (gain, out_w, *up_w)],
            *anywhere(earlier),
        ],
        out_specs=[narrow, narrow, narrow, whole((8, width))],
        out_shape=[
            jax.ShapeDtypeStruct((rows, width), F32),
            jax.ShapeDtypeStruct((rows, width), BF),
            jax.ShapeDtypeStruct((rows, width), BF),
            jax.ShapeDtypeStruct((8, width), F32),
        ],
        compiler_params=params(),
        cost_estimate=cost(2 * rows * width * (wide + width), 28e6),
        name="up_back",
    )(up_low, two, normed, scale, gain, out_w, *up_w, *earlier)


def attention_back_kernel(pattern, project_ref, probs_ref, g_ref, out_ref, sums_ref):
    width = g_ref.shape[2]
    half = g_ref.shape[1] // 2
    scale = HD ** (-0.5)
    lanes = lax.broadcasted_iota(jnp.int32, (half, 2 * HD), 1) < HD

    def pair(i, carry):
        base = i * (2 * HD)
        q_cols, k_cols, v_cols = (pl.ds(pl.multiple_of(j * width + base, 128), 2 * HD) for j in range(3))
        for b in range(2):
            rows = pl.ds(b * half, half)
            q = project_ref[0, rows, q_cols]
            g = g_ref[0, rows, q_cols]
            grads = []
            for h in range(2):
                mine = lanes if h == 0 else jnp.logical_not(lanes)
                met = jnp.where(pattern[2 * i + h] == 1, 1 - b, b)
                off = pl.ds(pl.multiple_of(met * half, half), half)
                k = project_ref[0, off, k_cols]
                v = project_ref[0, off, v_cols]
                p = probs_ref[0, 2 * i + h, b]
                wide = p.astype(F32)
                gp = dot_nt(jnp.where(mine, g, jnp.zeros_like(g)), v)
                inner = jnp.sum(wide * gp, axis=-1, keepdims=True)
                gs = (wide * (gp - inner)).astype(BF)
                grads.append(dot(gs, k))
                dk = (dot_tn(gs, q) * scale).astype(BF)
                dv = dot_tn(p, g).astype(BF)
                out_ref[0, off, k_cols] = jnp.where(mine, dk, out_ref[0, off, k_cols])
                out_ref[0, off, v_cols] = jnp.where(mine, dv, out_ref[0, off, v_cols])
            out_ref[0, rows, q_cols] = (jnp.where(lanes, *grads) * scale).astype(BF)
        return carry

    lax.fori_loop(0, H // 2, pair, 0)

    @pl.when(pl.program_id(0) == 0)
    def _():
        sums_ref[...] = jnp.zeros_like(sums_ref)

    sums_ref[...] += jnp.sum(out_ref[0].astype(F32), axis=0, keepdims=True)


def attention_back(project, probs, grad_mixed, pattern, earlier):
    n, length, width3 = project.shape
    width = width3 // 3
    half = length // 2
    units = n * H * 2 * half * half
    return pl.pallas_call(
        without(attention_back_kernel, 4, len(earlier)),
        grid_spec=pltpu.PrefetchScalarGridSpec(
            num_scalar_prefetch=1,
            grid=(n,),
            in_specs=[
                pl.BlockSpec((1, length, width3), lambda s, *_: (s, 0, 0)),
                pl.BlockSpec((1, H, 2, half, half), lambda s, *_: (s, 0, 0, 0, 0)),
                pl.BlockSpec((1, length, width), lambda s, *_: (s, 0, 0)),
                *anywhere(earlier),
            ],
            out_specs=[
                pl.BlockSpec((1, length, width3), lambda s, *_: (s, 0, 0)),
                whole((1, width3)),
            ],
        ),
        out_shape=[
            jax.ShapeDtypeStruct((n, length, width3), BF),
            jax.ShapeDtypeStruct((1, width3), F32),
        ],
        compiler_params=params(),
        cost_estimate=cost(8 * units * HD * 4, 20e6),
        name="attention_back",
    )(pattern, project, probs, grad_mixed, *earlier)


def tokens_kernel(one_ref, project_ref, w_ref, out_ref):
    out_ref[...] = (one_ref[...] + dot_nt(project_ref[...], w_ref[...])).astype(BF).reshape(out_ref.shape)


def tokens_back(one, grad_project, weight, piece, length, earlier, tile=256):
    rows, width = one.shape
    return pl.pallas_call(
        without(tokens_kernel, 3, len(earlier)),
        grid=(rows // tile,),
        in_specs=[
            rows_of(tile, width),
            rows_of(tile, grad_project.shape[1]),
            whole(weight.shape),
            *anywhere(earlier),
        ],
        out_specs=given(tile, piece, length, width),
        out_shape=jax.ShapeDtypeStruct((length // piece, rows // length, piece, width), BF),
        compiler_params=params(),
        cost_estimate=cost(2 * rows * width * grad_project.shape[1], 14e6),
        name="tokens_back",
    )(one, grad_project, weight, *earlier)


def core_swap(a):
    return lax.ppermute(a, "fsdp", [(i, i ^ 1) for i in range(lax.axis_size("fsdp"))])


def z_shift(a, k):
    n = lax.axis_size("dp")
    return lax.ppermute(a, "dp", [(i, (i + k) % n) for i in range(n)])


def z_pieces(a):
    return [a] + [z_shift(a, k) for k in range(1, lax.axis_size("dp"))]


def hop(a, away):
    return lax.ppermute(a, "fsdp", [(i, i ^ (2 * away)) for i in range(lax.axis_size("fsdp"))])


def plane_pieces(a):
    return [a] + [hop(a, away) for away in (1, 2, 3)]


def z_parts(a):
    n = lax.axis_size("dp")
    me = lax.axis_index("dp")
    return [lax.dynamic_index_in_dim(a, lax.rem(me + k, n), 0, False) for k in range(n)]


def z_scatter(parts):
    return [parts[0]] + [z_shift(a, k) for k, a in enumerate(parts) if k]


def total(parts):
    value = parts[0].astype(F32)
    for part in parts[1:]:
        value = value + part.astype(F32)
    return value


def after(a, *earlier):
    return lax.optimization_barrier((a, *earlier))[0]


def plane_exchange(a):
    size = lax.axis_size("fsdp")
    groups = [list(range(c, size, 2)) for c in range(2)]
    return lax.all_to_all(a, "fsdp", 0, 0, tiled=True, axis_index_groups=groups)


def by_plane(part):
    depth, plane = lax.axis_size("dp"), lax.axis_size("fsdp") // 2
    return jnp.transpose(part.reshape(depth, plane, -1, part.shape[1]), (1, 0, 2, 3))


def core_order(core, own, other, axis):
    return jnp.where(core == 0, jnp.concatenate([own, other], axis), jnp.concatenate([other, own], axis))


def half_of(a, which):
    wide = a.shape[1] // 2
    return lax.dynamic_slice_in_dim(a, which * wide, wide, 1)


def with_other_core(mine, spots, rows):
    return Pieces([mine, [core_swap(a) for a in mine]], spots, rows)


def plane_spots(depth):
    return [[(away, k) for k in range(depth)] for away in range(4)]


def finish(core, total):
    rows = total.shape[0] // 2
    own = lax.dynamic_slice_in_dim(total, core * rows, rows, 0)
    other = core_swap(lax.dynamic_slice_in_dim(total, (1 - core) * rows, rows, 0))
    return core_order(core, own, other, 1)


def summed(a):
    return jnp.sum(a.astype(F32), axis=0)


def hops(parts):
    return [parts[0]] + [hop(a, away) for away, a in enumerate(parts) if away]


def local(tokens, cotangent, key_mask, seq_lengths, block_pattern, deal_order, *shards):
    qkv_s, out_s, up_s, down_s = shards[:4]
    fsdp, depth = lax.axis_size("fsdp"), lax.axis_size("dp")
    devices, plane = fsdp * depth, fsdp // 2
    me = lax.axis_index("fsdp")
    core = lax.rem(me, 2)
    count, piece, width = tokens.shape
    per = count // fsdp
    length = piece * fsdp
    flat = (per * length, width)
    rows = 2 * qkv_s.shape[0]
    fast = rows % 16 == 0 and plane == 4 and depth % 2 == 0
    place = jnp.stack([core, me // 2, lax.axis_index("dp")]).astype(jnp.int32)
    sizes = (plane, depth)

    def deal(a):
        return lax.all_to_all(a, "fsdp", split_axis=0, concat_axis=1, tiled=True)

    def give(a):
        return lax.all_to_all(a, "fsdp", 0, 0, tiled=True).reshape(count, piece, width)

    slot = -(-shards[7].shape[0] // 128) * 128
    vectors = jnp.stack([jnp.pad(v.astype(F32), (0, slot - v.shape[0])) for v in shards[4:]]).reshape(-1)
    n_vec = vectors.shape[0]
    marks = key_mask.reshape(fsdp, per * piece)
    own = jnp.concatenate([vectors, seq_lengths.astype(F32)])
    notes = jnp.concatenate([marks.astype(F32), jnp.broadcast_to(own[None], (fsdp, own.shape[0]))], 1)
    notes = lax.all_to_all(notes, "fsdp", 0, 0, tiled=True)
    marks = notes[:, : per * piece].reshape(fsdp, per, piece).transpose(1, 0, 2).reshape(per, length)
    by_slot = notes[:, per * piece + n_vec :].T.reshape(-1).astype(jnp.int32)
    own_ids = me * per + jnp.arange(per, dtype=jnp.int32)
    own_lengths = jnp.sum(jnp.where(deal_order[0][None, :] == own_ids[:, None], by_slot[None, :], 0), axis=1)
    positions = jnp.arange(length, dtype=jnp.int32)
    valid = ((marks > 0.5) & (positions[None, :] < own_lengths[:, None])).astype(F32)
    valid = valid.reshape(per, 2, 1, length // 2)
    every = notes[:, per * piece : per * piece + n_vec].astype(BF)
    x3 = deal(after(tokens, notes))
    folds = up_s.shape[1] // width
    own = jnp.concatenate([out_s] + [up_s[:, j * width : (j + 1) * width] for j in range(folds)] + [down_s], 0)
    ffn_w = lax.all_gather(own[None], BOTH, axis=0, tiled=True)
    n = out_s.shape[0]
    out_w, *up_w = (ffn_w[:, j * n : (j + 1) * n].reshape(width, width) for j in range(1 + folds))
    down_w = ffn_w[:, (1 + folds) * n :].reshape(-1, width)
    if fast:
        chip = core_order(core, half_of(qkv_s, core), core_swap(half_of(qkv_s, 1 - core)), 0)
        every = jnp.pad(every, ((0, 8), (0, chip.shape[1] - n_vec)))
        first = z_pieces(jnp.concatenate([chip, every], 0))
        every = jnp.stack([a[rows : rows + fsdp, :n_vec] for a in first], 1)
        first = plane_pieces(jnp.stack([a[:rows] for a in first]))
        qkv_w = with_other_core(first, plane_spots(depth), rows)
        every = jnp.concatenate([every[:, :1], every[:, :0:-1]], 1)
        turn = lax.rem(depth - place[2], depth)
        every = lax.dynamic_slice_in_dim(jnp.concatenate([every, every], 1), turn, depth, 1)
        every = jnp.transpose(every, (1, 0, 2)).reshape(devices, n_vec)
    else:
        qkv_w = lax.all_gather(qkv_s, BOTH, axis=0, tiled=True)
        every = lax.all_gather(every, "dp", axis=0, tiled=True)
    every = every.astype(F32)
    lens = [s.shape[0] for s in shards[4:]]
    starts = [sum(lens[:i]) for i in range(len(lens))]
    query_b, value_b, out_b, up_b, down_b, attn_gain, attn_shift, ffn_gain, ffn_shift = (
        every[:, i * slot : i * slot + n].reshape(1, -1) for i, n in enumerate(lens)
    )

    g3 = deal(after(cotangent, x3, *(first if fast else ())))

    bias_all = jnp.concatenate([query_b, jnp.zeros_like(query_b), value_b], 1)
    project, mixed, probs, qkv_w = qkv_attention(place, block_pattern, x3, bias_all, valid, qkv_w, sizes)
    mixed = mixed.reshape(flat)
    x = x3.reshape(flat)
    normed, scale, hidden_low, active, slope = out_up(
        mixed, x, jnp.concatenate([out_b, attn_gain, attn_shift]), up_b, out_w, up_w
    )
    vecs = jnp.concatenate([attn_gain, attn_shift, down_b, ffn_gain, ffn_shift])
    output, grad_two, down_low, up_low, ffn_sums, grad_up_b = down_and_back(
        active, slope, normed, g3.reshape(flat), vecs, down_w, piece, length
    )
    output = give(output)

    up_gate = attention_gate = tokens_gate = ()
    if fast:
        down_sent = dot_tn(active, half_of(down_low, 1 - core)).astype(BF)
        up_sent = dot_tn(hidden_low, half_of(up_low, 1 - core)).astype(BF)
        down_part = total([dot_tn(active, half_of(down_low, core)), core_swap(down_sent)]).astype(BF)
        down_part = tie(by_plane(down_part), output)
        up_kept = total([dot_tn(hidden_low, half_of(up_low, core)), core_swap(up_sent)]).astype(BF)
        up_gate = (down_part, up_kept)
        down_part = plane_exchange(down_part)
    grad_one, out_low, grad_mixed, attn_sums = up_back(
        up_low, grad_two, normed, scale, attn_gain, out_w, up_w, up_gate
    )
    early = jnp.concatenate([attn_sums[2:3], ffn_sums[2:3], attn_sums[:2], ffn_sums[:2]], 0)
    early = jnp.transpose(early.reshape(6, devices, -1), (1, 0, 2)).reshape(devices, -1)
    early = jnp.concatenate([early, grad_up_b.reshape(devices, -1)], 1)
    if fast:
        early = (early + core_swap(early)).reshape(depth, plane, 2, -1).astype(BF)
        early = jnp.pad(early, ((0, 0), (0, 0), (0, 0), (0, 3 * width // 2 - early.shape[3])))
        out_sent = dot_tn(mixed, half_of(out_low, 1 - core)).astype(BF)
        out_kept = total([dot_tn(mixed, half_of(out_low, core)), core_swap(out_sent)]).astype(BF)
        up_part = by_plane(jnp.concatenate([up_kept, out_kept], 1))
        down_part = summed(tie(down_part, up_part)).astype(BF)
        down_part = jnp.concatenate([down_part[:, i * rows : (i + 1) * rows] for i in range(4)], 2)
        up_part = tie(up_part, down_part)
        attention_gate = (early, up_part, down_part)
        up_part = plane_exchange(up_part)
    grad_project, bias_sums = attention_back(
        project, probs, grad_mixed.reshape(per, length, width), block_pattern, attention_gate
    )
    grad_project = grad_project.reshape(per * length, 3 * width)
    if fast:
        up_part = summed(tie(up_part, grad_project)).astype(BF)
        up_part = jnp.concatenate([up_part, tie(down_part, bias_sums)], 2)
        grad_project = tie(grad_project, up_part)
        qkv_sent = dot_tn(x, half_of(grad_project, 1 - core)).astype(BF)
        biases = (bias_sums + core_swap(bias_sums)).reshape(2, -1).astype(BF)
        qkv_kept = total([dot_tn(x, half_of(grad_project, core)), core_swap(qkv_sent)]).astype(BF)
        wide = qkv_kept.shape[1]
        biases = jnp.pad(biases, ((0, 4), (0, 0)))
        extra = jnp.concatenate([early, jnp.broadcast_to(biases, (depth, plane, *biases.shape))], 2)
        qkv_part = jnp.concatenate([qkv_kept.reshape(depth, plane, rows, wide), extra], 2)
        qkv_part = [lax.dynamic_index_in_dim(qkv_part, place[1] ^ away, 1, False) for away in range(plane)]
        tokens_gate = (up_part, *qkv_part)
        qkv_part = hops(qkv_part)
    grad_tokens = tokens_back(grad_one, grad_project, qkv_w, piece, length, tokens_gate)
    if fast:
        cut = up_s.shape[1] // 2
        up_part = summed(tie(lax.all_to_all(up_part, "dp", 0, 0, tiled=True), grad_tokens))
        down_part = up_part[:, cut + width // 2 :].reshape(rows, 4, width // 2)
        down_part = jnp.transpose(down_part, (1, 0, 2)).reshape(4 * rows, width // 2)
        grad_down_w = finish(core, down_part)
        grad_up_w = finish(core, up_part[:, :cut])
        grad_out_w = finish(core, up_part[:, cut : cut + width // 2])
        qkv_part = [qkv_part[0]] + [tie(a, grad_tokens) for a in qkv_part[1:]]
        grad_tokens = give(tie(grad_tokens, up_part))
        last = total(z_scatter(z_parts(total(qkv_part).astype(BF))))
        grad_qkv_w = finish(core, last[:rows])
        biases = last[rows + 2 : rows + 4].reshape(-1)
        at = (place[2] * fsdp + me) * lens[0]
        vector = jnp.concatenate(
            [
                lax.dynamic_slice_in_dim(biases, at, lens[0], 0),
                lax.dynamic_slice_in_dim(biases, at + 2 * width, lens[0], 0),
                lax.dynamic_index_in_dim(last[rows : rows + 2], core, 0, False)[: sum(lens) - 2 * lens[0]],
            ]
        )
    else:
        grad_tokens = give(grad_tokens)
        late = jnp.concatenate([bias_sums[:, :width], bias_sums[:, 2 * width :]], 0)
        late = jnp.transpose(late.reshape(2, devices, -1), (1, 0, 2)).reshape(devices, -1)
        laid = jnp.concatenate([late, early], 1)
        grads = (dot_tn(x, grad_project), dot_tn(mixed, out_low), dot_tn(hidden_low, up_low))
        grads = (*grads, dot_tn(active, down_low), laid)
        grad_qkv_w, grad_out_w, grad_up_w, grad_down_w, vector = (
            lax.psum_scatter(w.astype(BF), BOTH, scatter_dimension=0, tiled=True).astype(F32) for w in grads
        )
        vector = vector.reshape(-1)
    vectors_out, at = [], 0
    for n in [lens[0]] * 8 + [lens[3]]:
        vectors_out.append(vector[at : at + n])
        at += n
    vectors_out = [vectors_out[i] for i in (0, 1, 2, 8, 3, 4, 5, 6, 7)]
    return (output, grad_tokens, grad_qkv_w, grad_out_w, grad_up_w, grad_down_w, *vectors_out)


def solution(mesh):
    rows = P(BOTH, None)
    vec = P(BOTH)
    in_specs = (
        P("dp", "fsdp", None),
        P("dp", "fsdp", None),
        P("dp", "fsdp"),
        vec,
        P(),
        P("dp", None),
        *([rows] * 4),
        *([vec] * 9),
    )
    out_specs = (P("dp", "fsdp", None), P("dp", "fsdp", None), *([rows] * 4), *([vec] * 9))
    return jax.shard_map(local, mesh=mesh, in_specs=in_specs, out_specs=out_specs, check_vma=False)
```

```python
import functools

import jax
import jax.numpy as jnp
from jax import lax
from jax.experimental import pallas as pl
from jax.experimental.pallas import tpu as pltpu
from jax.sharding import PartitionSpec as P

H = 12
HD = 64
EPSILON = 1e-12
NEGATIVE = -1e30
BF = jnp.bfloat16
F32 = jnp.float32
VMEM_LIMIT = 56 * 1024 * 1024
BOTH = ("dp", "fsdp")
WEIGHT = 1


def dot(a, b):
    return jnp.dot(a, b, preferred_element_type=F32)


def dot_nt(a, b):
    return lax.dot_general(a, b, (((1,), (1,)), ((), ())), preferred_element_type=F32)


def dot_tn(a, b):
    return lax.dot_general(a, b, (((0,), (0,)), ((), ())), preferred_element_type=F32)


def whole(shape):
    return pl.BlockSpec(shape, lambda *_: (0,) * len(shape), pipeline_mode=pl.Buffered(1))


def params():
    return pltpu.CompilerParams(vmem_limit_bytes=VMEM_LIMIT)


def cost(flops, size, exps=0):
    return pl.CostEstimate(flops=int(flops * WEIGHT), bytes_accessed=int(size * WEIGHT), transcendentals=int(exps * WEIGHT))


class Pieces:
    def __init__(self, halves, spots, rows):
        self.halves, self.spots, self.rows = halves, spots, rows

    def arrays(self):
        return [a for half in self.halves for a in half]

    def specs(self):
        return [whole(a.shape) for a in self.arrays()]

    def put(self, place, refs, start, wide, out_ref):
        core, plane_at, depth_at, plane, depth = place
        each = len(refs) // 2
        for side, part in ((core, refs[:each]), (1 - core, refs[each:])):
            cols = pl.ds(pl.multiple_of(side * wide, 128), wide)
            for ref, spots in zip(part, self.spots):
                for i, (away, back) in enumerate(spots):
                    chip = lax.rem(depth_at + depth - back, depth) * plane + (plane_at ^ away)
                    rows = pl.ds(pl.multiple_of(chip * self.rows, 16), self.rows)
                    out_ref[rows, cols] = ref[i, :, start : start + wide]


def without(kernel, first, count):
    return lambda *refs: kernel(*refs[:first], *refs[first + count :])


def anywhere(arrays):
    return [pl.BlockSpec(memory_space=pl.ANY)] * len(arrays)


def tie(a, *earlier):
    return pl.pallas_call(
        lambda *refs: None,
        in_specs=anywhere((a, *earlier)),
        out_specs=pl.BlockSpec(memory_space=pl.ANY),
        out_shape=jax.ShapeDtypeStruct(a.shape, a.dtype),
        input_output_aliases={0: 0},
        compiler_params=params(),
        cost_estimate=cost(0, 0),
        name="tie",
    )(a, *earlier)


def place_of(place_ref, plane, depth):
    return place_ref[0], place_ref[1], place_ref[2], plane, depth


def load_weight(pieces, sizes, place_ref, refs, start, wide, out_ref):
    if pieces is None:
        out_ref[...] = refs[0][:, start : start + out_ref.shape[1]]
    else:
        pieces.put(place_of(place_ref, *sizes), refs, start, wide, out_ref)


def attention_kernel(pieces, sizes, n_pieces, place_ref, pattern, x_ref, b_ref, valid_ref, *refs):
    w_in, (project_ref, mixed_ref, probs_ref, w_ref) = refs[:n_pieces], refs[n_pieces:]
    width = x_ref.shape[2]
    half = x_ref.shape[1] // 2

    @pl.when(pl.program_id(0) == 0)
    def _():
        load_weight(pieces, sizes, place_ref, w_in, 0, 3 * width // 2, w_ref)

    x = x_ref[0]
    for part in range(3):
        cols = slice(part * width, (part + 1) * width)
        value = dot(x, w_ref[:, cols]) + b_ref[:, cols]
        project_ref[0, :, cols] = value.astype(BF)
    lanes = lax.broadcasted_iota(jnp.int32, (half, 2 * HD), 1) < HD

    def pair(i, carry):
        base = i * (2 * HD)
        for b in range(2):
            rows = pl.ds(b * half, half)
            q = project_ref[0, rows, pl.ds(pl.multiple_of(base, 128), 2 * HD)] * jnp.asarray(HD ** (-0.5), BF)
            outs = []
            for h in range(2):
                met = jnp.where(pattern[2 * i + h] == 1, 1 - b, b)
                off = pl.ds(pl.multiple_of(met * half, half), half)
                k = project_ref[0, off, pl.ds(pl.multiple_of(width + base, 128), 2 * HD)]
                v = project_ref[0, off, pl.ds(pl.multiple_of(2 * width + base, 128), 2 * HD)]
                own = jnp.where(lanes if h == 0 else jnp.logical_not(lanes), q, jnp.zeros_like(q))
                scores = jnp.where(valid_ref[0, met] > 0.0, dot_nt(own, k), NEGATIVE)
                e = jnp.exp(scores - jnp.max(scores, axis=-1, keepdims=True))
                p = (e * (1.0 / jnp.sum(e, axis=-1, keepdims=True))).astype(BF)
                probs_ref[0, 2 * i + h, b] = p
                outs.append(dot(p, v))
            mixed_ref[0, rows, pl.ds(pl.multiple_of(base, 128), 2 * HD)] = jnp.where(lanes, *outs).astype(BF)
        return carry

    lax.fori_loop(0, H // 2, pair, 0)


def qkv_attention(place, pattern, x3, bias, valid, pieces, sizes):
    n, length, width = x3.shape
    half = length // 2
    arrays = pieces.arrays() if isinstance(pieces, Pieces) else [pieces]
    specs = [whole(a.shape) for a in arrays]
    units = n * H * 2 * half * half
    return pl.pallas_call(
        functools.partial(
            attention_kernel, pieces if isinstance(pieces, Pieces) else None, sizes, len(arrays)
        ),
        grid_spec=pltpu.PrefetchScalarGridSpec(
            num_scalar_prefetch=2,
            grid=(n,),
            in_specs=[
                pl.BlockSpec((1, length, width), lambda s, *_: (s, 0, 0)),
                whole((1, 3 * width)),
                pl.BlockSpec((1, 2, 1, half), lambda s, *_: (s, 0, 0, 0)),
                *specs,
            ],
            out_specs=[
                pl.BlockSpec((1, length, 3 * width), lambda s, *_: (s, 0, 0)),
                pl.BlockSpec((1, length, width), lambda s, *_: (s, 0, 0)),
                pl.BlockSpec((1, H, 2, half, half), lambda s, *_: (s, 0, 0, 0, 0)),
                whole((width, 3 * width)),
            ],
        ),
        out_shape=[
            jax.ShapeDtypeStruct((n, length, 3 * width), BF),
            jax.ShapeDtypeStruct((n, length, width), BF),
            jax.ShapeDtypeStruct((n, H, 2, half, half), BF),
            jax.ShapeDtypeStruct((width, 3 * width), BF),
        ],
        compiler_params=params(),
        cost_estimate=cost(6 * n * length * width * width + 4 * units * HD * 4, 22e6, units),
        name="qkv_attention",
    )(place, pattern, x3, bias, valid, *arrays)


def norm(residual):
    centre = residual - jnp.mean(residual, axis=-1, keepdims=True)
    scale = lax.rsqrt(jnp.mean(centre * centre, axis=-1, keepdims=True) + EPSILON)
    return centre * scale, scale


def norm_back(normed, scale, gained):
    inner = jnp.mean(gained * normed, axis=-1, keepdims=True)
    return scale * (gained - jnp.mean(gained, axis=-1, keepdims=True) - normed * inner)


def up_kernel(chunk, mixed_ref, x_ref, vec_ref, up_b_ref, out_w_ref, *refs):
    up_w, (normed_ref, scale_ref, low_ref, act_ref, slope_ref) = refs[:-5], refs[-5:]
    width = x_ref.shape[1]
    normed, scale = norm(x_ref[...].astype(F32) + dot(mixed_ref[...], out_w_ref[...]) + vec_ref[0:1])
    normed_ref[...] = normed
    scale_ref[...] = scale
    low = (normed * vec_ref[1:2] + vec_ref[2:3]).astype(BF)
    low_ref[...] = low
    for j, up_w_ref in enumerate(up_w):
        for start in range(0, width, chunk):
            cols = slice(j * width + start, j * width + start + chunk)
            u = dot(low, up_w_ref[:, start : start + chunk]) + up_b_ref[:, cols]
            phi = 0.5 + 0.5 * lax.erf(u * (2.0 ** -0.5))
            density = jnp.exp(-0.5 * u * u) * 0.3989422804014327
            act_ref[:, cols] = (u * phi).astype(BF)
            slope_ref[:, cols] = (phi + u * density).astype(BF)


def rows_of(tile, width):
    return pl.BlockSpec((tile, width), lambda i, *_: (i, 0))


def out_up(mixed, x, vecs, up_b, out_w, up_w, tile=256, chunk=384):
    rows, width = x.shape
    wide = up_b.shape[1]
    return pl.pallas_call(
        functools.partial(up_kernel, chunk),
        grid=(rows // tile,),
        in_specs=[
            rows_of(tile, width),
            rows_of(tile, width),
            *[whole(a.shape) for a in (vecs, up_b, out_w, *up_w)],
        ],
        out_specs=[
            rows_of(tile, width),
            rows_of(tile, 1),
            rows_of(tile, width),
            rows_of(tile, wide),
            rows_of(tile, wide),
        ],
        out_shape=[
            jax.ShapeDtypeStruct((rows, width), F32),
            jax.ShapeDtypeStruct((rows, 1), F32),
            jax.ShapeDtypeStruct((rows, width), BF),
            jax.ShapeDtypeStruct((rows, wide), BF),
            jax.ShapeDtypeStruct((rows, wide), BF),
        ],
        compiler_params=params(),
        cost_estimate=cost(2 * rows * width * (width + wide), 38e6, rows * wide),
        name="out_up",
    )(mixed, x, vecs, up_b, out_w, *up_w)


def down_kernel(act_ref, slope_ref, normed_ref, g_ref, vec_ref, w_ref, *refs):
    out_ref, two_ref, down_low_ref, up_low_ref, sums_ref, up_sum_ref = refs
    width = normed_ref.shape[1]

    @pl.when(pl.program_id(0) == 0)
    def _():
        sums_ref[...] = jnp.zeros_like(sums_ref)
        up_sum_ref[...] = jnp.zeros_like(up_sum_ref)

    hidden = normed_ref[...] * vec_ref[0:1] + vec_ref[1:2]
    normed, scale = norm(hidden + dot(act_ref[...], w_ref[...]) + vec_ref[2:3])
    out_ref[...] = (normed * vec_ref[3:4] + vec_ref[4:5]).astype(BF).reshape(out_ref.shape)
    g = g_ref[...].reshape(normed_ref.shape).astype(F32)
    two = norm_back(normed, scale, g * vec_ref[3:4])
    two_ref[...] = two
    low = two.astype(BF)
    down_low_ref[...] = low
    sums_ref[0:1] += jnp.sum(g * normed, axis=0, keepdims=True)
    sums_ref[1:2] += jnp.sum(g, axis=0, keepdims=True)
    sums_ref[2:3] += jnp.sum(low.astype(F32), axis=0, keepdims=True)
    for start in range(0, w_ref.shape[0], width):
        cols = slice(start, start + width)
        up_low = (dot_nt(low, w_ref[cols, :]) * slope_ref[:, cols].astype(F32)).astype(BF)
        up_low_ref[:, cols] = up_low
        up_sum_ref[:, cols] += jnp.sum(up_low.astype(F32), axis=0, keepdims=True)


def given(tile, piece, length, width):
    return pl.BlockSpec(
        (tile // piece, 1, piece, width), lambda i, *_: (lax.rem(i, length // tile), i // (length // tile), 0, 0)
    )


def down_and_back(active, slope, normed, g, vecs, down_w, piece, length, tile=256):
    rows, width = normed.shape
    wide = active.shape[1]
    return pl.pallas_call(
        down_kernel,
        grid=(rows // tile,),
        in_specs=[
            rows_of(tile, wide),
            rows_of(tile, wide),
            rows_of(tile, width),
            given(tile, piece, length, width),
            whole(vecs.shape),
            whole(down_w.shape),
        ],
        out_specs=[
            given(tile, piece, length, width),
            rows_of(tile, width),
            rows_of(tile, width),
            rows_of(tile, wide),
            whole((8, width)),
            whole((1, wide)),
        ],
        out_shape=[
            jax.ShapeDtypeStruct((length // piece, rows // length, piece, width), BF),
            jax.ShapeDtypeStruct((rows, width), F32),
            jax.ShapeDtypeStruct((rows, width), BF),
            jax.ShapeDtypeStruct((rows, wide), BF),
            jax.ShapeDtypeStruct((8, width), F32),
            jax.ShapeDtypeStruct((1, wide), F32),
        ],
        compiler_params=params(),
        cost_estimate=cost(4 * rows * width * wide, 38e6),
        name="down_and_back",
    )(active, slope, normed, g, vecs, down_w)


def up_back_kernel(up_low_ref, two_ref, normed_ref, scale_ref, gain_ref, out_w_ref, *refs):
    up_w, (one_ref, low_ref, mixed_ref, sums_ref) = refs[:-4], refs[-4:]
    width = two_ref.shape[1]

    @pl.when(pl.program_id(0) == 0)
    def _():
        sums_ref[...] = jnp.zeros_like(sums_ref)

    hidden = two_ref[...]
    for j, up_w_ref in enumerate(up_w):
        hidden = hidden + dot_nt(up_low_ref[:, j * width : (j + 1) * width], up_w_ref[...])
    normed = normed_ref[...]
    one = norm_back(normed, scale_ref[...], hidden * gain_ref[...])
    one_ref[...] = one
    low = one.astype(BF)
    low_ref[...] = low
    mixed_ref[...] = dot_nt(low, out_w_ref[...]).astype(BF)
    sums_ref[0:1] += jnp.sum(hidden * normed, axis=0, keepdims=True)
    sums_ref[1:2] += jnp.sum(hidden, axis=0, keepdims=True)
    sums_ref[2:3] += jnp.sum(low.astype(F32), axis=0, keepdims=True)


def up_back(up_low, two, normed, scale, gain, out_w, up_w, earlier, tile=256):
    rows, wide = up_low.shape
    width = two.shape[1]
    narrow = rows_of(tile, width)
    return pl.pallas_call(
        without(up_back_kernel, 6 + len(up_w), len(earlier)),
        grid=(rows // tile,),
        in_specs=[
            rows_of(tile, wide),
            narrow,
            narrow,
            rows_of(tile, 1),
            *[whole(a.shape) for a in (gain, out_w, *up_w)],
            *anywhere(earlier),
        ],
        out_specs=[narrow, narrow, narrow, whole((8, width))],
        out_shape=[
            jax.ShapeDtypeStruct((rows, width), F32),
            jax.ShapeDtypeStruct((rows, width), BF),
            jax.ShapeDtypeStruct((rows, width), BF),
            jax.ShapeDtypeStruct((8, width), F32),
        ],
        compiler_params=params(),
        cost_estimate=cost(2 * rows * width * (wide + width), 28e6),
        name="up_back",
    )(up_low, two, normed, scale, gain, out_w, *up_w, *earlier)


def attention_back_kernel(pattern, project_ref, probs_ref, g_ref, out_ref, sums_ref):
    width = g_ref.shape[2]
    half = g_ref.shape[1] // 2
    scale = HD ** (-0.5)
    lanes = lax.broadcasted_iota(jnp.int32, (half, 2 * HD), 1) < HD

    def pair(i, carry):
        base = i * (2 * HD)
        q_cols, k_cols, v_cols = (pl.ds(pl.multiple_of(j * width + base, 128), 2 * HD) for j in range(3))
        for b in range(2):
            rows = pl.ds(b * half, half)
            q = project_ref[0, rows, q_cols]
            g = g_ref[0, rows, q_cols]
            grads = []
            for h in range(2):
                mine = lanes if h == 0 else jnp.logical_not(lanes)
                met = jnp.where(pattern[2 * i + h] == 1, 1 - b, b)
                off = pl.ds(pl.multiple_of(met * half, half), half)
                k = project_ref[0, off, k_cols]
                v = project_ref[0, off, v_cols]
                p = probs_ref[0, 2 * i + h, b]
                wide = p.astype(F32)
                gp = dot_nt(jnp.where(mine, g, jnp.zeros_like(g)), v)
                inner = jnp.sum(wide * gp, axis=-1, keepdims=True)
                gs = (wide * (gp - inner)).astype(BF)
                grads.append(dot(gs, k))
                dk = (dot_tn(gs, q) * scale).astype(BF)
                dv = dot_tn(p, g).astype(BF)
                out_ref[0, off, k_cols] = jnp.where(mine, dk, out_ref[0, off, k_cols])
                out_ref[0, off, v_cols] = jnp.where(mine, dv, out_ref[0, off, v_cols])
            out_ref[0, rows, q_cols] = (jnp.where(lanes, *grads) * scale).astype(BF)
        return carry

    lax.fori_loop(0, H // 2, pair, 0)

    @pl.when(pl.program_id(0) == 0)
    def _():
        sums_ref[...] = jnp.zeros_like(sums_ref)

    sums_ref[...] += jnp.sum(out_ref[0].astype(F32), axis=0, keepdims=True)


def attention_back(project, probs, grad_mixed, pattern, earlier):
    n, length, width3 = project.shape
    width = width3 // 3
    half = length // 2
    units = n * H * 2 * half * half
    return pl.pallas_call(
        without(attention_back_kernel, 4, len(earlier)),
        grid_spec=pltpu.PrefetchScalarGridSpec(
            num_scalar_prefetch=1,
            grid=(n,),
            in_specs=[
                pl.BlockSpec((1, length, width3), lambda s, *_: (s, 0, 0)),
                pl.BlockSpec((1, H, 2, half, half), lambda s, *_: (s, 0, 0, 0, 0)),
                pl.BlockSpec((1, length, width), lambda s, *_: (s, 0, 0)),
                *anywhere(earlier),
            ],
            out_specs=[
                pl.BlockSpec((1, length, width3), lambda s, *_: (s, 0, 0)),
                whole((1, width3)),
            ],
        ),
        out_shape=[
            jax.ShapeDtypeStruct((n, length, width3), BF),
            jax.ShapeDtypeStruct((1, width3), F32),
        ],
        compiler_params=params(),
        cost_estimate=cost(8 * units * HD * 4, 20e6),
        name="attention_back",
    )(pattern, project, probs, grad_mixed, *earlier)


def tokens_kernel(one_ref, project_ref, w_ref, out_ref):
    out_ref[...] = (one_ref[...] + dot_nt(project_ref[...], w_ref[...])).astype(BF).reshape(out_ref.shape)


def tokens_back(one, grad_project, weight, piece, length, earlier, tile=256):
    rows, width = one.shape
    return pl.pallas_call(
        without(tokens_kernel, 3, len(earlier)),
        grid=(rows // tile,),
        in_specs=[
            rows_of(tile, width),
            rows_of(tile, grad_project.shape[1]),
            whole(weight.shape),
            *anywhere(earlier),
        ],
        out_specs=given(tile, piece, length, width),
        out_shape=jax.ShapeDtypeStruct((length // piece, rows // length, piece, width), BF),
        compiler_params=params(),
        cost_estimate=cost(2 * rows * width * grad_project.shape[1], 14e6),
        name="tokens_back",
    )(one, grad_project, weight, *earlier)


def core_swap(a):
    return lax.ppermute(a, "fsdp", [(i, i ^ 1) for i in range(lax.axis_size("fsdp"))])


def z_shift(a, k):
    n = lax.axis_size("dp")
    return lax.ppermute(a, "dp", [(i, (i + k) % n) for i in range(n)])


def z_pieces(a):
    return [a] + [z_shift(a, k) for k in range(1, lax.axis_size("dp"))]


def hop(a, away):
    return lax.ppermute(a, "fsdp", [(i, i ^ (2 * away)) for i in range(lax.axis_size("fsdp"))])


def plane_pieces(a):
    return [a] + [hop(a, away) for away in (1, 2, 3)]


def z_parts(a):
    n = lax.axis_size("dp")
    me = lax.axis_index("dp")
    return [lax.dynamic_index_in_dim(a, lax.rem(me + k, n), 0, False) for k in range(n)]


def z_scatter(parts):
    return [parts[0]] + [z_shift(a, k) for k, a in enumerate(parts) if k]


def total(parts):
    value = parts[0].astype(F32)
    for part in parts[1:]:
        value = value + part.astype(F32)
    return value


def after(a, *earlier):
    return lax.optimization_barrier((a, *earlier))[0]


def plane_exchange(a):
    size = lax.axis_size("fsdp")
    groups = [list(range(c, size, 2)) for c in range(2)]
    return lax.all_to_all(a, "fsdp", 0, 0, tiled=True, axis_index_groups=groups)


def by_plane(part):
    depth, plane = lax.axis_size("dp"), lax.axis_size("fsdp") // 2
    return jnp.transpose(part.reshape(depth, plane, -1, part.shape[1]), (1, 0, 2, 3))


def core_order(core, own, other, axis):
    return jnp.where(core == 0, jnp.concatenate([own, other], axis), jnp.concatenate([other, own], axis))


def half_of(a, which):
    wide = a.shape[1] // 2
    return lax.dynamic_slice_in_dim(a, which * wide, wide, 1)


def with_other_core(mine, spots, rows):
    return Pieces([mine, [core_swap(a) for a in mine]], spots, rows)


def plane_spots(depth):
    return [[(away, k) for k in range(depth)] for away in range(4)]


def finish(core, total):
    rows = total.shape[0] // 2
    own = lax.dynamic_slice_in_dim(total, core * rows, rows, 0)
    other = core_swap(lax.dynamic_slice_in_dim(total, (1 - core) * rows, rows, 0))
    return core_order(core, own, other, 1)


def summed(a):
    return jnp.sum(a.astype(F32), axis=0)


def hops(parts):
    return [parts[0]] + [hop(a, away) for away, a in enumerate(parts) if away]


def local(tokens, cotangent, key_mask, seq_lengths, block_pattern, deal_order, *shards):
    qkv_s, out_s, up_s, down_s = shards[:4]
    fsdp, depth = lax.axis_size("fsdp"), lax.axis_size("dp")
    devices, plane = fsdp * depth, fsdp // 2
    me = lax.axis_index("fsdp")
    core = lax.rem(me, 2)
    count, piece, width = tokens.shape
    per = count // fsdp
    length = piece * fsdp
    flat = (per * length, width)
    rows = 2 * qkv_s.shape[0]
    fast = rows % 16 == 0 and plane == 4 and depth % 2 == 0
    place = jnp.stack([core, me // 2, lax.axis_index("dp")]).astype(jnp.int32)
    sizes = (plane, depth)

    def deal(a):
        return lax.all_to_all(a, "fsdp", split_axis=0, concat_axis=1, tiled=True)

    def give(a):
        return lax.all_to_all(a, "fsdp", 0, 0, tiled=True).reshape(count, piece, width)

    slot = -(-shards[7].shape[0] // 128) * 128
    vectors = jnp.stack([jnp.pad(v.astype(F32), (0, slot - v.shape[0])) for v in shards[4:]]).reshape(-1)
    n_vec = vectors.shape[0]
    marks = key_mask.reshape(fsdp, per * piece)
    own = jnp.concatenate([vectors, seq_lengths.astype(F32)])
    notes = jnp.concatenate([marks.astype(F32), jnp.broadcast_to(own[None], (fsdp, own.shape[0]))], 1)
    notes = lax.all_to_all(notes, "fsdp", 0, 0, tiled=True)
    marks = notes[:, : per * piece].reshape(fsdp, per, piece).transpose(1, 0, 2).reshape(per, length)
    by_slot = notes[:, per * piece + n_vec :].T.reshape(-1).astype(jnp.int32)
    own_ids = me * per + jnp.arange(per, dtype=jnp.int32)
    own_lengths = jnp.sum(jnp.where(deal_order[0][None, :] == own_ids[:, None], by_slot[None, :], 0), axis=1)
    positions = jnp.arange(length, dtype=jnp.int32)
    valid = ((marks > 0.5) & (positions[None, :] < own_lengths[:, None])).astype(F32)
    valid = valid.reshape(per, 2, 1, length // 2)
    every = notes[:, per * piece : per * piece + n_vec].astype(BF)
    x3 = deal(after(tokens, notes))
    folds = up_s.shape[1] // width
    own = jnp.concatenate([out_s] + [up_s[:, j * width : (j + 1) * width] for j in range(folds)] + [down_s], 0)
    ffn_w = lax.all_gather(own[None], BOTH, axis=0, tiled=True)
    n = out_s.shape[0]
    out_w, *up_w = (ffn_w[:, j * n : (j + 1) * n].reshape(width, width) for j in range(1 + folds))
    down_w = ffn_w[:, (1 + folds) * n :].reshape(-1, width)
    if fast:
        chip = core_order(core, half_of(qkv_s, core), core_swap(half_of(qkv_s, 1 - core)), 0)
        every = jnp.pad(every, ((0, 8), (0, chip.shape[1] - n_vec)))
        first = z_pieces(jnp.concatenate([chip, every], 0))
        every = jnp.stack([a[rows : rows + fsdp, :n_vec] for a in first], 1)
        first = plane_pieces(jnp.stack([a[:rows] for a in first]))
        qkv_w = with_other_core(first, plane_spots(depth), rows)
        every = jnp.concatenate([every[:, :1], every[:, :0:-1]], 1)
        turn = lax.rem(depth - place[2], depth)
        every = lax.dynamic_slice_in_dim(jnp.concatenate([every, every], 1), turn, depth, 1)
        every = jnp.transpose(every, (1, 0, 2)).reshape(devices, n_vec)
    else:
        qkv_w = lax.all_gather(qkv_s, BOTH, axis=0, tiled=True)
        every = lax.all_gather(every, "dp", axis=0, tiled=True)
    every = every.astype(F32)
    lens = [s.shape[0] for s in shards[4:]]
    starts = [sum(lens[:i]) for i in range(len(lens))]
    query_b, value_b, out_b, up_b, down_b, attn_gain, attn_shift, ffn_gain, ffn_shift = (
        every[:, i * slot : i * slot + n].reshape(1, -1) for i, n in enumerate(lens)
    )


    bias_all = jnp.concatenate([query_b, jnp.zeros_like(query_b), value_b], 1)
    project, mixed, probs, qkv_w = qkv_attention(place, block_pattern, x3, bias_all, valid, qkv_w, sizes)
    mixed = mixed.reshape(flat)
    x = x3.reshape(flat)
    g = lax.all_to_all(tie(cotangent, mixed), "fsdp", 0, 0, tiled=True)
    normed, scale, hidden_low, active, slope = out_up(
        mixed, x, jnp.concatenate([out_b, attn_gain, attn_shift]), up_b, out_w, up_w
    )
    g = tie(g, active).reshape(fsdp, per, piece, width)
    vecs = jnp.concatenate([attn_gain, attn_shift, down_b, ffn_gain, ffn_shift])
    output, grad_two, down_low, up_low, ffn_sums, grad_up_b = down_and_back(
        active, slope, normed, g, vecs, down_w, piece, length
    )
    if not fast:
        output = give(output)

    up_gate = attention_gate = tokens_gate = ()
    if fast:
        down_sent = dot_tn(active, half_of(down_low, 1 - core)).astype(BF)
        up_sent = dot_tn(hidden_low, half_of(up_low, 1 - core)).astype(BF)
        down_part = total([dot_tn(active, half_of(down_low, core)), core_swap(down_sent)]).astype(BF)
        down_part = by_plane(down_part)
        up_kept = total([dot_tn(hidden_low, half_of(up_low, core)), core_swap(up_sent)]).astype(BF)
        up_gate = (down_part, up_kept)
        down_part = plane_exchange(down_part)
    grad_one, out_low, grad_mixed, attn_sums = up_back(
        up_low, grad_two, normed, scale, attn_gain, out_w, up_w, up_gate
    )
    early = jnp.concatenate([attn_sums, ffn_sums], 0)
    early = jnp.transpose(early.reshape(early.shape[0], devices, -1), (1, 0, 2)).reshape(devices, -1)
    early = jnp.concatenate([early, grad_up_b.reshape(devices, -1)], 1)
    if fast:
        early = (early + core_swap(early)).reshape(depth, plane, 2, -1).astype(BF)
        early = jnp.pad(early, ((0, 0), (0, 0), (0, 0), (0, 3 * width // 2 - early.shape[3])))
        out_sent = dot_tn(mixed, half_of(out_low, 1 - core)).astype(BF)
        out_kept = total([dot_tn(mixed, half_of(out_low, core)), core_swap(out_sent)]).astype(BF)
        up_part = by_plane(jnp.concatenate([up_kept, out_kept], 1))
        down_part = summed(tie(down_part, up_part)).astype(BF)
        down_part = jnp.concatenate([down_part[:, i * rows : (i + 1) * rows] for i in range(4)], 2)
        up_part = tie(up_part, down_part)
        attention_gate = (early, up_part, down_part)
        up_part = plane_exchange(up_part)
    grad_project, bias_sums = attention_back(
        project, probs, grad_mixed.reshape(per, length, width), block_pattern, attention_gate
    )
    grad_project = grad_project.reshape(per * length, 3 * width)
    if fast:
        up_part = summed(tie(up_part, grad_project)).astype(BF)
        output = give(tie(output, up_part))
        up_part = z_parts(jnp.concatenate([up_part, tie(down_part, bias_sums)], 2))
        grad_project = tie(grad_project, *up_part)
        qkv_sent = dot_tn(x, half_of(grad_project, 1 - core)).astype(BF)
        biases = (bias_sums + core_swap(bias_sums)).reshape(2, -1).astype(BF)
        qkv_kept = total([dot_tn(x, half_of(grad_project, core)), core_swap(qkv_sent)]).astype(BF)
        wide = qkv_kept.shape[1]
        biases = jnp.pad(biases, ((0, 4), (0, 0)))
        extra = jnp.concatenate([early, jnp.broadcast_to(biases, (depth, plane, *biases.shape))], 2)
        qkv_part = jnp.concatenate([qkv_kept.reshape(depth, plane, rows, wide), extra], 2)
        qkv_part = [lax.dynamic_index_in_dim(qkv_part, place[1] ^ away, 1, False) for away in range(plane)]
        up_part = z_scatter(up_part)
        tokens_gate = tuple(qkv_part)
        qkv_part = hops(qkv_part)
    grad_tokens = tokens_back(grad_one, grad_project, qkv_w, piece, length, tokens_gate)
    if fast:
        cut = up_s.shape[1] // 2
        up_part = total([up_part[0]] + [tie(a, grad_tokens) for a in up_part[1:]])
        down_part = up_part[:, cut + width // 2 :].reshape(rows, 4, width // 2)
        down_part = jnp.transpose(down_part, (1, 0, 2)).reshape(4 * rows, width // 2)
        grad_down_w = finish(core, down_part)
        grad_up_w = finish(core, up_part[:, :cut])
        grad_out_w = finish(core, up_part[:, cut : cut + width // 2])
        qkv_part = [qkv_part[0]] + [tie(a, grad_tokens) for a in qkv_part[1:]]
        output = tie(output, grad_tokens)
        grad_tokens = give(tie(grad_tokens, output))
        last = total(z_scatter(z_parts(total(qkv_part).astype(BF))))
        grad_qkv_w = finish(core, last[:rows])
        biases = last[rows + 2 : rows + 4].reshape(-1)
        at = (place[2] * fsdp + me) * lens[0]
        vector = jnp.concatenate(
            [
                lax.dynamic_slice_in_dim(biases, at, lens[0], 0),
                lax.dynamic_slice_in_dim(biases, at + 2 * width, lens[0], 0),
                lax.dynamic_index_in_dim(last[rows : rows + 2], core, 0, False)[: 16 * lens[0] + lens[3]],
            ]
        )
    else:
        grad_tokens = give(grad_tokens)
        late = jnp.concatenate([bias_sums[:, :width], bias_sums[:, 2 * width :]], 0)
        late = jnp.transpose(late.reshape(2, devices, -1), (1, 0, 2)).reshape(devices, -1)
        laid = jnp.concatenate([late, early], 1)
        grads = (dot_tn(x, grad_project), dot_tn(mixed, out_low), dot_tn(hidden_low, up_low))
        grads = (*grads, dot_tn(active, down_low), laid)
        grad_qkv_w, grad_out_w, grad_up_w, grad_down_w, vector = (
            lax.psum_scatter(w.astype(BF), BOTH, scatter_dimension=0, tiled=True).astype(F32) for w in grads
        )
        vector = vector.reshape(-1)
    n = lens[0]
    spots = (0, 1, 4, 18, 12, 2, 3, 10, 11)
    vectors_out = [vector[i * n : i * n + size] for i, size in zip(spots, lens)]
    return (output, grad_tokens, grad_qkv_w, grad_out_w, grad_up_w, grad_down_w, *vectors_out)


def solution(mesh):
    rows = P(BOTH, None)
    vec = P(BOTH)
    in_specs = (
        P("dp", "fsdp", None),
        P("dp", "fsdp", None),
        P("dp", "fsdp"),
        vec,
        P(),
        P("dp", None),
        *([rows] * 4),
        *([vec] * 9),
    )
    out_specs = (P("dp", "fsdp", None), P("dp", "fsdp", None), *([rows] * 4), *([vec] * 9))
    return jax.shard_map(local, mesh=mesh, in_specs=in_specs, out_specs=out_specs, check_vma=False)
```

```python
import functools

import jax
import jax.numpy as jnp
from jax import lax
from jax.experimental import pallas as pl
from jax.experimental.pallas import tpu as pltpu
from jax.sharding import PartitionSpec as P

H = 12
HD = 64
EPSILON = 1e-12
NEGATIVE = -1e30
BF = jnp.bfloat16
F32 = jnp.float32
VMEM_LIMIT = 56 * 1024 * 1024
BOTH = ("dp", "fsdp")
WEIGHT = 1


def dot(a, b):
    return jnp.dot(a, b, preferred_element_type=F32)


def dot_nt(a, b):
    return lax.dot_general(a, b, (((1,), (1,)), ((), ())), preferred_element_type=F32)


def dot_tn(a, b):
    return lax.dot_general(a, b, (((0,), (0,)), ((), ())), preferred_element_type=F32)


def whole(shape):
    return pl.BlockSpec(shape, lambda *_: (0,) * len(shape), pipeline_mode=pl.Buffered(1))


def params():
    return pltpu.CompilerParams(vmem_limit_bytes=VMEM_LIMIT)


def cost(flops, size, exps=0):
    return pl.CostEstimate(flops=int(flops * WEIGHT), bytes_accessed=int(size * WEIGHT), transcendentals=int(exps * WEIGHT))


class Pieces:
    def __init__(self, halves, spots, rows):
        self.halves, self.spots, self.rows = halves, spots, rows

    def arrays(self):
        return [a for half in self.halves for a in half]

    def specs(self):
        return [whole(a.shape) for a in self.arrays()]

    def put(self, place, refs, start, wide, out_ref):
        core, plane_at, depth_at, plane, depth = place
        each = len(refs) // 2
        for side, part in ((core, refs[:each]), (1 - core, refs[each:])):
            cols = pl.ds(pl.multiple_of(side * wide, 128), wide)
            for ref, spots in zip(part, self.spots):
                for i, (away, back) in enumerate(spots):
                    chip = lax.rem(depth_at + depth - back, depth) * plane + (plane_at ^ away)
                    rows = pl.ds(pl.multiple_of(chip * self.rows, 16), self.rows)
                    out_ref[rows, cols] = ref[i, :, start : start + wide]


def without(kernel, first, count):
    return lambda *refs: kernel(*refs[:first], *refs[first + count :])


def anywhere(arrays):
    return [pl.BlockSpec(memory_space=pl.ANY)] * len(arrays)


def tie(a, *earlier):
    return pl.pallas_call(
        lambda *refs: None,
        in_specs=anywhere((a, *earlier)),
        out_specs=pl.BlockSpec(memory_space=pl.ANY),
        out_shape=jax.ShapeDtypeStruct(a.shape, a.dtype),
        input_output_aliases={0: 0},
        compiler_params=params(),
        cost_estimate=cost(0, 0),
        name="tie",
    )(a, *earlier)


def place_of(place_ref, plane, depth):
    return place_ref[0], place_ref[1], place_ref[2], plane, depth


def load_weight(pieces, sizes, place_ref, refs, start, wide, out_ref):
    if pieces is None:
        out_ref[...] = refs[0][:, start : start + out_ref.shape[1]]
    else:
        pieces.put(place_of(place_ref, *sizes), refs, start, wide, out_ref)


def attention_kernel(pieces, sizes, n_pieces, place_ref, pattern, x_ref, b_ref, valid_ref, *refs):
    w_in, (project_ref, mixed_ref, probs_ref, w_ref) = refs[:n_pieces], refs[n_pieces:]
    width = x_ref.shape[2]
    half = x_ref.shape[1] // 2

    @pl.when(pl.program_id(0) == 0)
    def _():
        load_weight(pieces, sizes, place_ref, w_in, 0, 3 * width // 2, w_ref)

    x = x_ref[0]
    for part in range(3):
        cols = slice(part * width, (part + 1) * width)
        value = dot(x, w_ref[:, cols]) + b_ref[:, cols]
        project_ref[0, :, cols] = value.astype(BF)
    lanes = lax.broadcasted_iota(jnp.int32, (half, 2 * HD), 1) < HD

    def pair(i, carry):
        base = i * (2 * HD)
        for b in range(2):
            rows = pl.ds(b * half, half)
            q = project_ref[0, rows, pl.ds(pl.multiple_of(base, 128), 2 * HD)] * jnp.asarray(HD ** (-0.5), BF)
            outs = []
            for h in range(2):
                met = jnp.where(pattern[2 * i + h] == 1, 1 - b, b)
                off = pl.ds(pl.multiple_of(met * half, half), half)
                k = project_ref[0, off, pl.ds(pl.multiple_of(width + base, 128), 2 * HD)]
                v = project_ref[0, off, pl.ds(pl.multiple_of(2 * width + base, 128), 2 * HD)]
                own = jnp.where(lanes if h == 0 else jnp.logical_not(lanes), q, jnp.zeros_like(q))
                scores = jnp.where(valid_ref[0, met] > 0.0, dot_nt(own, k), NEGATIVE)
                e = jnp.exp(scores - jnp.max(scores, axis=-1, keepdims=True))
                p = (e * (1.0 / jnp.sum(e, axis=-1, keepdims=True))).astype(BF)
                probs_ref[0, 2 * i + h, b] = p
                outs.append(dot(p, v))
            mixed_ref[0, rows, pl.ds(pl.multiple_of(base, 128), 2 * HD)] = jnp.where(lanes, *outs).astype(BF)
        return carry

    lax.fori_loop(0, H // 2, pair, 0)


def qkv_attention(place, pattern, x3, bias, valid, pieces, sizes):
    n, length, width = x3.shape
    half = length // 2
    arrays = pieces.arrays() if isinstance(pieces, Pieces) else [pieces]
    specs = [whole(a.shape) for a in arrays]
    units = n * H * 2 * half * half
    return pl.pallas_call(
        functools.partial(
            attention_kernel, pieces if isinstance(pieces, Pieces) else None, sizes, len(arrays)
        ),
        grid_spec=pltpu.PrefetchScalarGridSpec(
            num_scalar_prefetch=2,
            grid=(n,),
            in_specs=[
                pl.BlockSpec((1, length, width), lambda s, *_: (s, 0, 0)),
                whole((1, 3 * width)),
                pl.BlockSpec((1, 2, 1, half), lambda s, *_: (s, 0, 0, 0)),
                *specs,
            ],
            out_specs=[
                pl.BlockSpec((1, length, 3 * width), lambda s, *_: (s, 0, 0)),
                pl.BlockSpec((1, length, width), lambda s, *_: (s, 0, 0)),
                pl.BlockSpec((1, H, 2, half, half), lambda s, *_: (s, 0, 0, 0, 0)),
                whole((width, 3 * width)),
            ],
        ),
        out_shape=[
            jax.ShapeDtypeStruct((n, length, 3 * width), BF),
            jax.ShapeDtypeStruct((n, length, width), BF),
            jax.ShapeDtypeStruct((n, H, 2, half, half), BF),
            jax.ShapeDtypeStruct((width, 3 * width), BF),
        ],
        compiler_params=params(),
        cost_estimate=cost(6 * n * length * width * width + 4 * units * HD * 4, 22e6, units),
        name="qkv_attention",
    )(place, pattern, x3, bias, valid, *arrays)


def norm(residual):
    centre = residual - jnp.mean(residual, axis=-1, keepdims=True)
    scale = lax.rsqrt(jnp.mean(centre * centre, axis=-1, keepdims=True) + EPSILON)
    return centre * scale, scale


def norm_back(normed, scale, gained):
    inner = jnp.mean(gained * normed, axis=-1, keepdims=True)
    return scale * (gained - jnp.mean(gained, axis=-1, keepdims=True) - normed * inner)


def up_kernel(chunk, mixed_ref, x_ref, vec_ref, up_b_ref, out_w_ref, *refs):
    up_w, (normed_ref, scale_ref, low_ref, act_ref, slope_ref) = refs[:-5], refs[-5:]
    width = x_ref.shape[1]
    normed, scale = norm(x_ref[...].astype(F32) + dot(mixed_ref[...], out_w_ref[...]) + vec_ref[0:1])
    normed_ref[...] = normed
    scale_ref[...] = scale
    low = (normed * vec_ref[1:2] + vec_ref[2:3]).astype(BF)
    low_ref[...] = low
    for j, up_w_ref in enumerate(up_w):
        for start in range(0, width, chunk):
            cols = slice(j * width + start, j * width + start + chunk)
            u = dot(low, up_w_ref[:, start : start + chunk]) + up_b_ref[:, cols]
            phi = 0.5 + 0.5 * lax.erf(u * (2.0 ** -0.5))
            density = jnp.exp(-0.5 * u * u) * 0.3989422804014327
            act_ref[:, cols] = (u * phi).astype(BF)
            slope_ref[:, cols] = (phi + u * density).astype(BF)


def rows_of(tile, width):
    return pl.BlockSpec((tile, width), lambda i, *_: (i, 0))


def out_up(mixed, x, vecs, up_b, out_w, up_w, tile=256, chunk=384):
    rows, width = x.shape
    wide = up_b.shape[1]
    return pl.pallas_call(
        functools.partial(up_kernel, chunk),
        grid=(rows // tile,),
        in_specs=[
            rows_of(tile, width),
            rows_of(tile, width),
            *[whole(a.shape) for a in (vecs, up_b, out_w, *up_w)],
        ],
        out_specs=[
            rows_of(tile, width),
            rows_of(tile, 1),
            rows_of(tile, width),
            rows_of(tile, wide),
            rows_of(tile, wide),
        ],
        out_shape=[
            jax.ShapeDtypeStruct((rows, width), F32),
            jax.ShapeDtypeStruct((rows, 1), F32),
            jax.ShapeDtypeStruct((rows, width), BF),
            jax.ShapeDtypeStruct((rows, wide), BF),
            jax.ShapeDtypeStruct((rows, wide), BF),
        ],
        compiler_params=params(),
        cost_estimate=cost(2 * rows * width * (width + wide), 38e6, rows * wide),
        name="out_up",
    )(mixed, x, vecs, up_b, out_w, *up_w)


def chunks(w_ref):
    width = w_ref.shape[2]
    each = width // w_ref.shape[1]
    for i in range(w_ref.shape[0] // each):
        yield slice(i * width, (i + 1) * width), w_ref[i * each : (i + 1) * each].reshape(width, width)


def down_of(act_ref, w_ref):
    value = 0.0
    for cols, weight in chunks(w_ref):
        value = value + dot(act_ref[:, cols], weight)
    return value


def down_kernel(act_ref, slope_ref, normed_ref, g_ref, vec_ref, w_ref, *refs):
    out_ref, two_ref, down_low_ref, up_low_ref, sums_ref, up_sum_ref = refs
    width = normed_ref.shape[1]

    @pl.when(pl.program_id(0) == 0)
    def _():
        sums_ref[...] = jnp.zeros_like(sums_ref)
        up_sum_ref[...] = jnp.zeros_like(up_sum_ref)

    hidden = normed_ref[...] * vec_ref[0:1] + vec_ref[1:2]
    normed, scale = norm(hidden + down_of(act_ref, w_ref) + vec_ref[2:3])
    out_ref[...] = (normed * vec_ref[3:4] + vec_ref[4:5]).astype(BF).reshape(out_ref.shape)
    g = g_ref[...].reshape(normed_ref.shape).astype(F32)
    two = norm_back(normed, scale, g * vec_ref[3:4])
    two_ref[...] = two
    low = two.astype(BF)
    down_low_ref[...] = low
    sums_ref[0:1] += jnp.sum(g * normed, axis=0, keepdims=True)
    sums_ref[1:2] += jnp.sum(g, axis=0, keepdims=True)
    sums_ref[2:3] += jnp.sum(low.astype(F32), axis=0, keepdims=True)
    for cols, weight in chunks(w_ref):
        up_low = (dot_nt(low, weight) * slope_ref[:, cols].astype(F32)).astype(BF)
        up_low_ref[:, cols] = up_low
        up_sum_ref[:, cols] += jnp.sum(up_low.astype(F32), axis=0, keepdims=True)


def given(tile, piece, length, width):
    return pl.BlockSpec(
        (tile // piece, 1, piece, width), lambda i, *_: (lax.rem(i, length // tile), i // (length // tile), 0, 0)
    )


def down_and_back(active, slope, normed, g, vecs, down_w, piece, length, tile=256):
    rows, width = normed.shape
    wide = active.shape[1]
    return pl.pallas_call(
        down_kernel,
        grid=(rows // tile,),
        in_specs=[
            rows_of(tile, wide),
            rows_of(tile, wide),
            rows_of(tile, width),
            given(tile, piece, length, width),
            whole(vecs.shape),
            whole((down_w.shape[0], wide // down_w.shape[0], width)),
        ],
        out_specs=[
            given(tile, piece, length, width),
            rows_of(tile, width),
            rows_of(tile, width),
            rows_of(tile, wide),
            whole((8, width)),
            whole((1, wide)),
        ],
        out_shape=[
            jax.ShapeDtypeStruct((length // piece, rows // length, piece, width), BF),
            jax.ShapeDtypeStruct((rows, width), F32),
            jax.ShapeDtypeStruct((rows, width), BF),
            jax.ShapeDtypeStruct((rows, wide), BF),
            jax.ShapeDtypeStruct((8, width), F32),
            jax.ShapeDtypeStruct((1, wide), F32),
        ],
        compiler_params=params(),
        cost_estimate=cost(4 * rows * width * wide, 38e6),
        name="down_and_back",
    )(active, slope, normed, g, vecs, down_w)


def up_back_kernel(up_low_ref, two_ref, normed_ref, scale_ref, gain_ref, out_w_ref, *refs):
    up_w, (one_ref, low_ref, mixed_ref, sums_ref) = refs[:-4], refs[-4:]
    width = two_ref.shape[1]

    @pl.when(pl.program_id(0) == 0)
    def _():
        sums_ref[...] = jnp.zeros_like(sums_ref)

    hidden = two_ref[...]
    for j, up_w_ref in enumerate(up_w):
        hidden = hidden + dot_nt(up_low_ref[:, j * width : (j + 1) * width], up_w_ref[...])
    normed = normed_ref[...]
    one = norm_back(normed, scale_ref[...], hidden * gain_ref[...])
    one_ref[...] = one
    low = one.astype(BF)
    low_ref[...] = low
    mixed_ref[...] = dot_nt(low, out_w_ref[...]).astype(BF)
    sums_ref[0:1] += jnp.sum(hidden * normed, axis=0, keepdims=True)
    sums_ref[1:2] += jnp.sum(hidden, axis=0, keepdims=True)
    sums_ref[2:3] += jnp.sum(low.astype(F32), axis=0, keepdims=True)


def up_back(up_low, two, normed, scale, gain, out_w, up_w, earlier, tile=256):
    rows, wide = up_low.shape
    width = two.shape[1]
    narrow = rows_of(tile, width)
    return pl.pallas_call(
        without(up_back_kernel, 6 + len(up_w), len(earlier)),
        grid=(rows // tile,),
        in_specs=[
            rows_of(tile, wide),
            narrow,
            narrow,
            rows_of(tile, 1),
            *[whole(a.shape) for a in (gain, out_w, *up_w)],
            *anywhere(earlier),
        ],
        out_specs=[narrow, narrow, narrow, whole((8, width))],
        out_shape=[
            jax.ShapeDtypeStruct((rows, width), F32),
            jax.ShapeDtypeStruct((rows, width), BF),
            jax.ShapeDtypeStruct((rows, width), BF),
            jax.ShapeDtypeStruct((8, width), F32),
        ],
        compiler_params=params(),
        cost_estimate=cost(2 * rows * width * (wide + width), 28e6),
        name="up_back",
    )(up_low, two, normed, scale, gain, out_w, *up_w, *earlier)


def attention_back_kernel(pattern, project_ref, probs_ref, g_ref, out_ref, sums_ref):
    width = g_ref.shape[2]
    half = g_ref.shape[1] // 2
    scale = HD ** (-0.5)
    lanes = lax.broadcasted_iota(jnp.int32, (half, 2 * HD), 1) < HD

    def pair(i, carry):
        base = i * (2 * HD)
        q_cols, k_cols, v_cols = (pl.ds(pl.multiple_of(j * width + base, 128), 2 * HD) for j in range(3))
        for b in range(2):
            rows = pl.ds(b * half, half)
            q = project_ref[0, rows, q_cols]
            g = g_ref[0, rows, q_cols]
            grads = []
            for h in range(2):
                mine = lanes if h == 0 else jnp.logical_not(lanes)
                met = jnp.where(pattern[2 * i + h] == 1, 1 - b, b)
                off = pl.ds(pl.multiple_of(met * half, half), half)
                k = project_ref[0, off, k_cols]
                v = project_ref[0, off, v_cols]
                p = probs_ref[0, 2 * i + h, b]
                wide = p.astype(F32)
                gp = dot_nt(jnp.where(mine, g, jnp.zeros_like(g)), v)
                inner = jnp.sum(wide * gp, axis=-1, keepdims=True)
                gs = (wide * (gp - inner)).astype(BF)
                grads.append(dot(gs, k))
                dk = (dot_tn(gs, q) * scale).astype(BF)
                dv = dot_tn(p, g).astype(BF)
                out_ref[0, off, k_cols] = jnp.where(mine, dk, out_ref[0, off, k_cols])
                out_ref[0, off, v_cols] = jnp.where(mine, dv, out_ref[0, off, v_cols])
            out_ref[0, rows, q_cols] = (jnp.where(lanes, *grads) * scale).astype(BF)
        return carry

    lax.fori_loop(0, H // 2, pair, 0)

    @pl.when(pl.program_id(0) == 0)
    def _():
        sums_ref[...] = jnp.zeros_like(sums_ref)

    sums_ref[...] += jnp.sum(out_ref[0].astype(F32), axis=0, keepdims=True)


def attention_back(project, probs, grad_mixed, pattern, earlier):
    n, length, width3 = project.shape
    width = width3 // 3
    half = length // 2
    units = n * H * 2 * half * half
    return pl.pallas_call(
        without(attention_back_kernel, 4, len(earlier)),
        grid_spec=pltpu.PrefetchScalarGridSpec(
            num_scalar_prefetch=1,
            grid=(n,),
            in_specs=[
                pl.BlockSpec((1, length, width3), lambda s, *_: (s, 0, 0)),
                pl.BlockSpec((1, H, 2, half, half), lambda s, *_: (s, 0, 0, 0, 0)),
                pl.BlockSpec((1, length, width), lambda s, *_: (s, 0, 0)),
                *anywhere(earlier),
            ],
            out_specs=[
                pl.BlockSpec((1, length, width3), lambda s, *_: (s, 0, 0)),
                whole((1, width3)),
            ],
        ),
        out_shape=[
            jax.ShapeDtypeStruct((n, length, width3), BF),
            jax.ShapeDtypeStruct((1, width3), F32),
        ],
        compiler_params=params(),
        cost_estimate=cost(8 * units * HD * 4, 20e6),
        name="attention_back",
    )(pattern, project, probs, grad_mixed, *earlier)


def tokens_kernel(one_ref, project_ref, w_ref, out_ref):
    out_ref[...] = (one_ref[...] + dot_nt(project_ref[...], w_ref[...])).astype(BF).reshape(out_ref.shape)


def tokens_back(one, grad_project, weight, piece, length, earlier, tile=256):
    rows, width = one.shape
    return pl.pallas_call(
        without(tokens_kernel, 3, len(earlier)),
        grid=(rows // tile,),
        in_specs=[
            rows_of(tile, width),
            rows_of(tile, grad_project.shape[1]),
            whole(weight.shape),
            *anywhere(earlier),
        ],
        out_specs=given(tile, piece, length, width),
        out_shape=jax.ShapeDtypeStruct((length // piece, rows // length, piece, width), BF),
        compiler_params=params(),
        cost_estimate=cost(2 * rows * width * grad_project.shape[1], 14e6),
        name="tokens_back",
    )(one, grad_project, weight, *earlier)


def core_swap(a):
    return lax.ppermute(a, "fsdp", [(i, i ^ 1) for i in range(lax.axis_size("fsdp"))])


def z_shift(a, k):
    n = lax.axis_size("dp")
    return lax.ppermute(a, "dp", [(i, (i + k) % n) for i in range(n)])


def z_pieces(a):
    return [a] + [z_shift(a, k) for k in range(1, lax.axis_size("dp"))]


def hop(a, away):
    return lax.ppermute(a, "fsdp", [(i, i ^ (2 * away)) for i in range(lax.axis_size("fsdp"))])


def plane_pieces(a):
    return [a] + [hop(a, away) for away in (1, 2, 3)]


def z_parts(a):
    n = lax.axis_size("dp")
    me = lax.axis_index("dp")
    return [lax.dynamic_index_in_dim(a, lax.rem(me + k, n), 0, False) for k in range(n)]


def z_scatter(parts):
    return [parts[0]] + [z_shift(a, k) for k, a in enumerate(parts) if k]


def total(parts):
    value = parts[0].astype(F32)
    for part in parts[1:]:
        value = value + part.astype(F32)
    return value


def after(a, *earlier):
    return lax.optimization_barrier((a, *earlier))[0]


def plane_exchange(a):
    size = lax.axis_size("fsdp")
    groups = [list(range(c, size, 2)) for c in range(2)]
    return lax.all_to_all(a, "fsdp", 0, 0, tiled=True, axis_index_groups=groups)


def by_plane(part):
    depth, plane = lax.axis_size("dp"), lax.axis_size("fsdp") // 2
    return jnp.transpose(part.reshape(depth, plane, -1, part.shape[1]), (1, 0, 2, 3))


def core_order(core, own, other, axis):
    return jnp.where(core == 0, jnp.concatenate([own, other], axis), jnp.concatenate([other, own], axis))


def half_of(a, which):
    wide = a.shape[1] // 2
    return lax.dynamic_slice_in_dim(a, which * wide, wide, 1)


def with_other_core(mine, spots, rows):
    return Pieces([mine, [core_swap(a) for a in mine]], spots, rows)


def plane_spots(depth):
    return [[(away, k) for k in range(depth)] for away in range(4)]


def finish(core, total):
    rows = total.shape[0] // 2
    own = lax.dynamic_slice_in_dim(total, core * rows, rows, 0)
    other = core_swap(lax.dynamic_slice_in_dim(total, (1 - core) * rows, rows, 0))
    return core_order(core, own, other, 1)


def summed(a):
    return jnp.sum(a.astype(F32), axis=0)


def hops(parts):
    return [parts[0]] + [hop(a, away) for away, a in enumerate(parts) if away]


def local(tokens, cotangent, key_mask, seq_lengths, block_pattern, deal_order, *shards):
    qkv_s, out_s, up_s, down_s = shards[:4]
    fsdp, depth = lax.axis_size("fsdp"), lax.axis_size("dp")
    devices, plane = fsdp * depth, fsdp // 2
    me = lax.axis_index("fsdp")
    core = lax.rem(me, 2)
    count, piece, width = tokens.shape
    per = count // fsdp
    length = piece * fsdp
    flat = (per * length, width)
    rows = 2 * qkv_s.shape[0]
    fast = rows % 16 == 0 and plane == 4 and depth % 2 == 0
    place = jnp.stack([core, me // 2, lax.axis_index("dp")]).astype(jnp.int32)
    sizes = (plane, depth)

    def deal(a):
        return lax.all_to_all(a, "fsdp", split_axis=0, concat_axis=1, tiled=True)

    def give(a):
        return lax.all_to_all(a, "fsdp", 0, 0, tiled=True).reshape(count, piece, width)

    slot = -(-shards[7].shape[0] // 128) * 128
    vectors = jnp.stack([jnp.pad(v.astype(F32), (0, slot - v.shape[0])) for v in shards[4:]]).reshape(-1)
    n_vec = vectors.shape[0]
    marks = key_mask.reshape(fsdp, per * piece)
    own = jnp.concatenate([vectors, seq_lengths.astype(F32)])
    notes = jnp.concatenate([marks.astype(F32), jnp.broadcast_to(own[None], (fsdp, own.shape[0]))], 1)
    notes = lax.all_to_all(notes, "fsdp", 0, 0, tiled=True)
    marks = notes[:, : per * piece].reshape(fsdp, per, piece).transpose(1, 0, 2).reshape(per, length)
    by_slot = notes[:, per * piece + n_vec :].T.reshape(-1).astype(jnp.int32)
    own_ids = me * per + jnp.arange(per, dtype=jnp.int32)
    own_lengths = jnp.sum(jnp.where(deal_order[0][None, :] == own_ids[:, None], by_slot[None, :], 0), axis=1)
    positions = jnp.arange(length, dtype=jnp.int32)
    valid = ((marks > 0.5) & (positions[None, :] < own_lengths[:, None])).astype(F32)
    valid = valid.reshape(per, 2, 1, length // 2)
    every = notes[:, per * piece : per * piece + n_vec].astype(BF)
    x3 = deal(after(tokens, notes))
    folds = up_s.shape[1] // width
    own = jnp.concatenate([down_s, out_s] + [up_s[:, j * width : (j + 1) * width] for j in range(folds)], 0)
    down_w = ffn_w = lax.all_gather(own[None], BOTH, axis=0, tiled=True)
    n, m = out_s.shape[0], down_s.shape[0]
    out_w, *up_w = (ffn_w[:, m + j * n : m + (j + 1) * n].reshape(width, width) for j in range(1 + folds))
    if not fast:
        down_w = ffn_w[:, :m].reshape(-1, width, width)
    if fast:
        chip = core_order(core, half_of(qkv_s, core), core_swap(half_of(qkv_s, 1 - core)), 0)
        every = jnp.pad(every, ((0, 8), (0, chip.shape[1] - n_vec)))
        first = z_pieces(jnp.concatenate([chip, every], 0))
        every = jnp.stack([a[rows : rows + fsdp, :n_vec] for a in first], 1)
        first = plane_pieces(jnp.stack([a[:rows] for a in first]))
        qkv_w = with_other_core(first, plane_spots(depth), rows)
        every = jnp.concatenate([every[:, :1], every[:, :0:-1]], 1)
        turn = lax.rem(depth - place[2], depth)
        every = lax.dynamic_slice_in_dim(jnp.concatenate([every, every], 1), turn, depth, 1)
        every = jnp.transpose(every, (1, 0, 2)).reshape(devices, n_vec)
    else:
        qkv_w = lax.all_gather(qkv_s, BOTH, axis=0, tiled=True)
        every = lax.all_gather(every, "dp", axis=0, tiled=True)
    every = every.astype(F32)
    lens = [s.shape[0] for s in shards[4:]]
    starts = [sum(lens[:i]) for i in range(len(lens))]
    query_b, value_b, out_b, up_b, down_b, attn_gain, attn_shift, ffn_gain, ffn_shift = (
        every[:, i * slot : i * slot + n].reshape(1, -1) for i, n in enumerate(lens)
    )


    bias_all = jnp.concatenate([query_b, jnp.zeros_like(query_b), value_b], 1)
    project, mixed, probs, qkv_w = qkv_attention(place, block_pattern, x3, bias_all, valid, qkv_w, sizes)
    mixed = mixed.reshape(flat)
    x = x3.reshape(flat)
    g = lax.all_to_all(tie(cotangent, mixed), "fsdp", 0, 0, tiled=True)
    normed, scale, hidden_low, active, slope = out_up(
        mixed, x, jnp.concatenate([out_b, attn_gain, attn_shift]), up_b, out_w, up_w
    )
    g = tie(g, active).reshape(fsdp, per, piece, width)
    vecs = jnp.concatenate([attn_gain, attn_shift, down_b, ffn_gain, ffn_shift])
    output, grad_two, down_low, up_low, ffn_sums, grad_up_b = down_and_back(
        active, slope, normed, g, vecs, down_w, piece, length
    )
    if not fast:
        output = give(output)

    up_gate = attention_gate = tokens_gate = ()
    if fast:
        down_sent = dot_tn(active, half_of(down_low, 1 - core)).astype(BF)
        up_sent = dot_tn(hidden_low, half_of(up_low, 1 - core)).astype(BF)
        down_part = total([dot_tn(active, half_of(down_low, core)), core_swap(down_sent)]).astype(BF)
        down_part = by_plane(down_part)
        up_kept = total([dot_tn(hidden_low, half_of(up_low, core)), core_swap(up_sent)]).astype(BF)
        up_gate = (down_part, up_kept)
        down_part = plane_exchange(down_part)
    grad_one, out_low, grad_mixed, attn_sums = up_back(
        up_low, grad_two, normed, scale, attn_gain, out_w, up_w, up_gate
    )
    early = jnp.concatenate([attn_sums, ffn_sums], 0)
    early = jnp.transpose(early.reshape(early.shape[0], devices, -1), (1, 0, 2)).reshape(devices, -1)
    early = jnp.concatenate([early, grad_up_b.reshape(devices, -1)], 1)
    if fast:
        early = (early + core_swap(early)).reshape(depth, plane, 2, -1).astype(BF)
        early = jnp.pad(early, ((0, 0), (0, 0), (0, 0), (0, 3 * width // 2 - early.shape[3])))
        out_sent = dot_tn(mixed, half_of(out_low, 1 - core)).astype(BF)
        out_kept = total([dot_tn(mixed, half_of(out_low, core)), core_swap(out_sent)]).astype(BF)
        up_part = by_plane(jnp.concatenate([up_kept, out_kept], 1))
        down_part = summed(tie(down_part, up_part)).astype(BF)
        down_part = jnp.concatenate([down_part[:, i * rows : (i + 1) * rows] for i in range(4)], 2)
        up_part = tie(up_part, down_part)
        attention_gate = (early, up_part, down_part)
        up_part = plane_exchange(up_part)
    grad_project, bias_sums = attention_back(
        project, probs, grad_mixed.reshape(per, length, width), block_pattern, attention_gate
    )
    grad_project = grad_project.reshape(per * length, 3 * width)
    if fast:
        up_part = summed(tie(up_part, grad_project)).astype(BF)
        output = give(tie(output, up_part))
        up_part = z_parts(jnp.concatenate([up_part, tie(down_part, bias_sums)], 2))
        grad_project = tie(grad_project, *up_part)
        qkv_sent = dot_tn(x, half_of(grad_project, 1 - core)).astype(BF)
        biases = (bias_sums + core_swap(bias_sums)).reshape(2, -1).astype(BF)
        qkv_kept = total([dot_tn(x, half_of(grad_project, core)), core_swap(qkv_sent)]).astype(BF)
        wide = qkv_kept.shape[1]
        biases = jnp.pad(biases, ((0, 4), (0, 0)))
        extra = jnp.concatenate([early, jnp.broadcast_to(biases, (depth, plane, *biases.shape))], 2)
        qkv_part = jnp.concatenate([qkv_kept.reshape(depth, plane, rows, wide), extra], 2)
        qkv_part = [lax.dynamic_index_in_dim(qkv_part, place[1] ^ away, 1, False) for away in range(plane)]
        up_part = z_scatter(up_part)
        tokens_gate = tuple(qkv_part)
        qkv_part = hops(qkv_part)
    grad_tokens = tokens_back(grad_one, grad_project, qkv_w, piece, length, tokens_gate)
    if fast:
        cut = up_s.shape[1] // 2
        up_part = total([up_part[0]] + [tie(a, grad_tokens) for a in up_part[1:]])
        down_part = up_part[:, cut + width // 2 :].reshape(rows, 4, width // 2)
        down_part = jnp.transpose(down_part, (1, 0, 2)).reshape(4 * rows, width // 2)
        grad_down_w = finish(core, down_part)
        grad_up_w = finish(core, up_part[:, :cut])
        grad_out_w = finish(core, up_part[:, cut : cut + width // 2])
        qkv_part = [qkv_part[0]] + [tie(a, grad_tokens) for a in qkv_part[1:]]
        output = tie(output, grad_tokens)
        grad_tokens = give(tie(grad_tokens, output))
        last = total(z_scatter(z_parts(total(qkv_part).astype(BF))))
        grad_qkv_w = finish(core, last[:rows])
        biases = last[rows + 2 : rows + 4].reshape(-1)
        at = (place[2] * fsdp + me) * lens[0]
        vector = jnp.concatenate(
            [
                lax.dynamic_slice_in_dim(biases, at, lens[0], 0),
                lax.dynamic_slice_in_dim(biases, at + 2 * width, lens[0], 0),
                lax.dynamic_index_in_dim(last[rows : rows + 2], core, 0, False)[: 16 * lens[0] + lens[3]],
            ]
        )
    else:
        grad_tokens = give(grad_tokens)
        late = jnp.concatenate([bias_sums[:, :width], bias_sums[:, 2 * width :]], 0)
        late = jnp.transpose(late.reshape(2, devices, -1), (1, 0, 2)).reshape(devices, -1)
        laid = jnp.concatenate([late, early], 1)
        grads = (dot_tn(x, grad_project), dot_tn(mixed, out_low), dot_tn(hidden_low, up_low))
        grads = (*grads, dot_tn(active, down_low), laid)
        grad_qkv_w, grad_out_w, grad_up_w, grad_down_w, vector = (
            lax.psum_scatter(w.astype(BF), BOTH, scatter_dimension=0, tiled=True).astype(F32) for w in grads
        )
        vector = vector.reshape(-1)
    n = lens[0]
    spots = (0, 1, 4, 18, 12, 2, 3, 10, 11)
    vectors_out = [vector[i * n : i * n + size] for i, size in zip(spots, lens)]
    return (output, grad_tokens, grad_qkv_w, grad_out_w, grad_up_w, grad_down_w, *vectors_out)


def solution(mesh):
    rows = P(BOTH, None)
    vec = P(BOTH)
    in_specs = (
        P("dp", "fsdp", None),
        P("dp", "fsdp", None),
        P("dp", "fsdp"),
        vec,
        P(),
        P("dp", None),
        *([rows] * 4),
        *([vec] * 9),
    )
    out_specs = (P("dp", "fsdp", None), P("dp", "fsdp", None), *([rows] * 4), *([vec] * 9))
    return jax.shard_map(local, mesh=mesh, in_specs=in_specs, out_specs=out_specs, check_vma=False)
```
